512 devices in a mesh: dp: 16 (over x_lo, y), vocab: 32 (over x_hi, z, core).
Axes of the slice: x: 4 (x_hi: 2, x_lo: 2; x = x_hi * 2 + x_lo), y: 8, z: 8, core: 2. Of those that a mesh axis runs over, the one named last changes fastest.
Arguments:
- teacher_hidden: bfloat16 [384, 4608], P('dp', 'vocab'), may hold values from -6 to 6
- teacher_head: bfloat16 [4608, 131072], P(None, ('dp', 'vocab')), may hold values from -0.625 to 0.625
- student_hidden: bfloat16 [384, 2304], P('dp', 'vocab'), may hold values from -6 to 6
- student_gain: float32 [2304], replicated, may hold values from 0.5 to 1.5
- student_head: bfloat16 [2304, 131072], P(None, ('dp', 'vocab')), may hold values from -1 to 1
- token_mask: int32 [384], replicated, may hold values 0 or 1
Outputs:
- token_kl: float32 [384], replicated
- loss: float32 [], replicated
- grad_hidden: float32 [384, 2304], P('dp', 'vocab')
- grad_gain: float32 [2304], P('vocab')
The draws below stay inside these ranges and needn't reach their ends.
All inputs are finite; a program needn't handle non-finite values.
Results may differ from the reference program's by a relative error of at most 0.0053.
Values may be sent and summed in bfloat16 or wider, within the bound.
A program may use at most 64 MiB of HBM per device.

```python
import jax
import jax.numpy as jnp
from jax import lax

DT = 4608
DS = 2304
TOKENS = 384
VOCAB = 131072


def set_ends(entries, rng, least, top_value):
    dims = entries.shape
    spot = [jax.random.randint(jax.random.fold_in(rng, axis), (), 0, dims[axis]) for axis in range(len(dims))]
    entries = entries.at[tuple(spot)].set(least)
    longest = dims.index(max(dims))
    spot[longest] = (spot[longest] + 1) % dims[longest]
    return entries.at[tuple(spot)].set(top_value)


def block_scale(rng, extent, split, low, top_value):
    gain, own = 1.0, jax.random.fold_in(rng, 6)
    for position, parts in split:
        steps = jnp.exp(jax.random.uniform(jax.random.fold_in(own, position), (parts,), jnp.float32, low / len(split), top_value / len(split)))
        gain = gain * jnp.repeat(steps, extent[position] // parts).reshape([-1 if axis == position else 1 for axis in range(len(extent))])
    return gain


def centred(stream_key, extent, scale, bound, cuts=(), dtype=jnp.bfloat16):
    loudness = block_scale(stream_key, extent, cuts, -0.22, 0.18) if cuts else 1.0
    drawn = jax.random.normal(stream_key, extent, jnp.float32) * scale * loudness
    return jnp.minimum(jnp.maximum(drawn, -bound), bound).astype(dtype)


def setup_inputs(seed: int = 0) -> dict:
    arg_keys = jax.random.split(jax.random.key(seed), 7)
    return {
        "teacher_hidden": centred(arg_keys[0], (TOKENS, DT), 1.0, 6.0, ((0, 16), (1, 32))),
        "teacher_head": centred(arg_keys[1], (DT, VOCAB), (3.0 * DT ** -0.5), 0.625, ((1, 512),)),
        "student_hidden": centred(arg_keys[2], (TOKENS, DS), 1.0, 6.0, ((0, 16), (1, 32))),
        "student_gain": jnp.clip(1.0 + 0.1 * jax.random.normal(arg_keys[3], (DS,), jnp.float32), 0.5, 1.5),
        "student_head": centred(arg_keys[4], (DS, VOCAB), (3.0 * DS ** -0.5), 1.0, ((1, 512),)),
        "token_mask": set_ends((jax.random.randint(arg_keys[5], (TOKENS,), 0, 4) < 3).astype(jnp.int32), jax.random.fold_in(arg_keys[5], 1), 0, 1),
    }


def reference(teacher_hidden, teacher_head, student_hidden, student_gain, student_head, token_mask):
    xf = student_hidden.astype(jnp.float32)
    scale = jax.lax.rsqrt(lax.optimization_barrier(jnp.mean(xf * xf, axis=1)) + 1e-06)
    normed = (xf * scale[:, None] * student_gain[None, :]).astype(jnp.bfloat16)
    teach = 30.0 * jnp.tanh(jnp.dot(teacher_hidden, teacher_head, preferred_element_type=jnp.float32) / 30.0)
    pupil = 30.0 * jnp.tanh(jnp.dot(normed, student_head, preferred_element_type=jnp.float32) / 30.0)
    exp_teach = jnp.exp(teach - 30.0)
    exp_pupil = jnp.exp(pupil - 30.0)
    total_teach = lax.optimization_barrier(jnp.sum(exp_teach, axis=1))
    total_pupil = lax.optimization_barrier(jnp.sum(exp_pupil, axis=1))
    cross = lax.optimization_barrier(jnp.sum(exp_teach * (teach - pupil), axis=1))
    token_kl = cross / total_teach - jnp.log(total_teach) + jnp.log(total_pupil)
    maskf = token_mask.astype(jnp.float32)
    weight = maskf / jnp.maximum(jnp.sum(maskf), 1.0)
    loss = jnp.sum(weight * token_kl)
    dpupil = weight[:, None] * (exp_pupil / total_pupil[:, None] - exp_teach / total_teach[:, None])
    dpupil = (dpupil * (1.0 - (pupil / 30.0) ** 2)).astype(jnp.bfloat16)
    dnormed = jnp.dot(dpupil, student_head.T, preferred_element_type=jnp.float32)
    grad_gain = lax.optimization_barrier(jnp.sum(dnormed * xf * scale[:, None], axis=0))
    rowdot = lax.optimization_barrier(jnp.sum(dnormed * student_gain[None, :] * xf, axis=1))
    grad_hidden = student_gain[None, :] * dnormed * scale[:, None] - xf * (scale ** 3 * rowdot / DS)[:, None]
    return (token_kl, loss, grad_hidden, grad_gain)
```

```python
import jax
import jax.numpy as jnp
from jax import lax
from jax.experimental import pallas as pl
from jax.experimental.pallas import tpu as pltpu
from jax.sharding import PartitionSpec as P

F32, BF16 = jnp.float32, jnp.bfloat16
MESH = pl.DeviceIdType.MESH
N = 8
TOK, ROWS = 384, 24
TF, SF = 144, 72
SP = 80
VOC = 256
STOP = 99


def body(
    th, sh, gain, mask, wt_hbm, ws_hbm,
    kl_out, loss_out, gh_out, gg_out,
    wt, ws, wtt, wst, wsr, gb, pad_t, pad_s, piece, got, xt, xs, ns,
    ls, lt, pu, ep, qq, ql, et, dpu, s_own, s_sib, s_z, s_y, s_x, cols,
    g_own, g_out, g_in, r_out, r_in, e_out, e_in, f_out, f_in,
    w_sem, p_send, p_recv, h_send, h_recv, ring_send, ring_recv, sib_send, sib_recv,
    a_send, a_recv, z_send, z_recv, y_send, y_recv, x_send, x_recv,
    gs_send, gs_recv, rr_send, rr_recv, e_send, e_recv, f_send, f_recv,
):
    d, v = lax.axis_index("dp"), lax.axis_index("vocab")
    xl, y = d // N, d % N
    s, z, xh = v % 2, (v // 2) % N, v // (2 * N)
    first = s == 0
    p = jnp.where(first, z, y)
    q = jnp.where(first, y, z)

    def dev(xl, y, xh, z, s):
        return (xl * N + y, (xh * N + z) * 2 + s)

    def ring(place):
        return dev(xl, jnp.where(first, y, place), xh, jnp.where(first, place, z), s)

    def holder(m):
        a, j = m // N, m % N
        return dev(a, jnp.where(first, j, z), xh, jnp.where(first, z, j), s)

    def owner(m):
        return dev(m // N, m % N, xh, p, s)

    self_in = jnp.logical_or(first, y == z)
    right, left = ring((p + 1) % N), ring((p + N - 1) % N)
    sibling = dev(xl, y, xh, z, 1 - s)
    across = dev(1 - xl, y, 1 - xh, z, s)

    def remote(src, dst, send, recv, to):
        return pltpu.make_async_remote_copy(
            src_ref=src, dst_ref=dst, send_sem=send, recv_sem=recv, device_id=to, device_id_type=MESH
        )

    wt_copy = pltpu.make_async_copy(wt_hbm, wt, w_sem.at[0])
    ws_copy = pltpu.make_async_copy(ws_hbm, ws, w_sem.at[1])
    wt_copy.start()
    ws_copy.start()

    barrier = pltpu.get_barrier_semaphore()

    def tell(to):
        pl.semaphore_signal(barrier, inc=1, device_id=to, device_id_type=MESH)

    def greet(m, _):
        for who in (holder(m), owner(m)):
            @pl.when(jnp.logical_not(jnp.logical_and(who[0] == d, who[1] == v)))
            def _():
                tell(who)
        return 0

    lax.fori_loop(0, 2 * N, greet, 0)

    def greet_lines(j, _):
        tell(dev(xl, y, xh, (z + j) % N, s))
        tell(dev(xl, (y + j) % N, xh, z, s))
        return 0

    lax.fori_loop(1, N, greet_lines, 0)
    tell(sibling)
    for a, b in ((1 - xl, xh), (xl, 1 - xh), (1 - xl, 1 - xh)):
        tell(dev(a, y, b, z, s))

    pad_t[...] = jnp.zeros_like(pad_t)
    pad_s[...] = jnp.zeros_like(pad_s)
    pad_t[:, :TF] = th[...].astype(F32)
    pad_s[:, :SF] = sh[...].astype(F32)
    lane = lax.broadcasted_iota(jnp.int32, (ROWS, 128), 1)
    low = jnp.where(lane < TF - 128, pad_t[:, 128:256], pltpu.roll(pad_s[...], TF - 128, 1))
    piece[...] = jnp.concatenate([pad_t[:, :128], low], axis=0).astype(BF16)

    @pl.when(self_in)
    def _():
        got[d] = piece[...]

    pl.semaphore_wait(barrier, 4 * N - 2 * self_in.astype(jnp.int32) + 2 * (N - 1) + 4)

    def piece_send(m):
        return remote(piece, got.at[d], p_send.at[m], p_recv.at[d], holder(m))

    def away(m):
        who = holder(m)
        return jnp.logical_not(jnp.logical_and(who[0] == d, who[1] == v))

    def send_pieces(i, _):
        m = (d + 1 + i) % (2 * N)

        @pl.when(away(m))
        def _():
            piece_send(m).start()

        return 0

    lax.fori_loop(0, 2 * N, send_pieces, 0)

    for i in range(18):
        gb[i * 128:(i + 1) * 128, :] = jnp.broadcast_to(gain[i:i + 1, :], (128, 128)).T
    ws_copy.wait()

    def reorder(c, _):
        one = ws[pl.ds(pl.multiple_of(c * TF, 16), TF), :].astype(F32)
        two = ws[pl.ds(pl.multiple_of((N + c) * TF, 16), TF), :].astype(F32)
        wsr[c] = jnp.concatenate([one[:SF], two[:SF]], axis=0).astype(BF16)
        wsr[N + c] = jnp.concatenate([one[SF:], two[SF:]], axis=0).astype(BF16)
        return 0

    lax.fori_loop(0, N, reorder, 0)

    def turn_student(i):
        block = wsr[i * N:(i + 1) * N].reshape(N * TF, VOC)
        for j in range(9):
            wst[i, :, j * 128:(j + 1) * 128] = block[j * 128:(j + 1) * 128, :].T

    def turn_teacher(i):
        for j in range(9):
            at = (i * 9 + j) * 128
            wtt[i, :, j * 128:(j + 1) * 128] = wt[at:at + 128, :].T

    turn_student(0)
    turn_student(1)

    def wait_pieces(m, _):
        @pl.when(jnp.logical_not(jnp.logical_and(self_in, m == d)))
        def _():
            remote(piece, got.at[m], p_send.at[m], p_recv.at[m], sibling).wait_recv()

        return 0

    lax.fori_loop(0, 2 * N, wait_pieces, 0)

    pieces = [got[m].astype(F32) for m in range(2 * N)]
    upper = jnp.concatenate([t[:ROWS] for t in pieces], axis=0).T
    lower = jnp.concatenate([t[ROWS:] for t in pieces], axis=0).T
    tail = TF - 128
    mine_t, mine_s = (xh * N + p) * 2 + s, s * 2 * N + xh * N + p
    xt[mine_t] = jnp.concatenate([upper, lower[:tail]], axis=0).astype(BF16)
    xs[mine_s] = lower[tail:tail + SP].astype(BF16)

    def unit(core, place, other, teacher):
        half = 1 - xh if other else xh
        if teacher:
            return xt.at[(half * N + place) * 2 + core]
        return xs.at[core * 2 * N + half * N + place]

    sent = []

    def push(ref, send, recv, to):
        copy = remote(ref, ref, send, recv, to)
        copy.start()
        sent.append(copy)

    for kind in (0, 1):
        push(unit(s, p, 0, kind), h_send.at[kind], h_recv.at[kind], across)

    units = [(0, 0), (0, 1), (1, 0), (1, 1)]

    def to_ring(way, step, u, place):
        i = (way * 4 + step) * 4 + u
        push(unit(s, place, *units[u]), ring_send.at[i], ring_recv.at[i], (right, left)[way])

    def from_ring(way, step, u, place):
        i = (way * 4 + step) * 4 + u
        ref = unit(s, place, *units[u])
        remote(ref, ref, ring_send.at[i], ring_recv.at[i], sibling).wait_recv()

    def to_sibling(slot, u, place):
        i = slot * 4 + u
        push(unit(s, place, *units[u]), sib_send.at[i], sib_recv.at[i], sibling)

    def from_sibling(slot, u, place):
        i = slot * 4 + u
        ref = unit(1 - s, place, *units[u])
        remote(ref, ref, sib_send.at[i], sib_recv.at[i], sibling).wait_recv()

    def behind(place, way, step):
        return (place + (N - step if way == 0 else step)) % N

    for u, (other, kind) in enumerate(units):
        if other:
            ref = unit(s, p, other, kind)
            remote(ref, ref, h_send.at[kind], h_recv.at[kind], sibling).wait_recv()
        to_ring(0, 0, u, p)
        to_ring(1, 0, u, p)
        to_sibling(0, u, p)
        if u == 0:
            wt_copy.wait()
            turn_teacher(0)
    turn_teacher(1)

    for step in (1, 2, 3):
        for u, (other, kind) in enumerate(units):
            for way in (0, 1):
                place = behind(p, way, step)
                from_ring(way, step - 1, u, place)
                if step < 3 or other == way:
                    to_ring(way, step, u, place)
                to_sibling(way * 3 + step, u, place)
        if step < 3:
            turn_teacher(step + 1)

    far, sib_far = behind(p, 0, 4), behind(q, 0, 4)

    def last(kind):
        for way in (0, 1):
            u = units.index((way, kind))
            from_ring(way, 3, u, far)
            to_sibling(7, u, far)

    def all_from_sibling(kind):
        for other in (0, 1):
            u = units.index((other, kind))
            from_sibling(0, u, q)
            for step in (1, 2, 3):
                for way in (0, 1):
                    from_sibling(way * 3 + step, u, behind(q, way, step))
            from_sibling(7, u, sib_far)

    last(0)
    all_from_sibling(0)

    def squares(i, total):
        x = xs[i].astype(F32)
        for j in range(SF // 8):
            part = x[j * 8:(j + 1) * 8]
            total = total + part * part
        return total

    total = lax.fori_loop(0, 4 * N, squares, jnp.zeros((8, TOK), F32))
    scale = lax.rsqrt(jnp.sum(total, axis=0, keepdims=True) / (SF * 4 * N) + 1e-6)

    def normalise(i, _):
        core, c = i // N, i % N
        base = core * 2 * N + c
        for half in (0, 1):
            x = xs[base + half * N].astype(F32)[:SF]
            at = pl.multiple_of(((half * N + c) * 2 + core) * SF, 8)
            g = gb[pl.ds(at, SF), :]
            n = (x * scale) * jnp.concatenate([g, g, g], axis=1)
            if half == 0:
                head = n
        ns[i] = jnp.concatenate([head, n], axis=0).astype(BF16)
        return 0

    lax.fori_loop(0, 2 * N, normalise, 0)

    def dot(a, b):
        return jnp.dot(a, b, preferred_element_type=F32)

    ls[...] = dot(wst[0], ns[0:N].reshape(N * TF, TOK))
    ls[...] += dot(wst[1], ns[N:2 * N].reshape(N * TF, TOK))

    step_rows = 32

    def fold(x):
        out = x[0:8]
        for j in range(1, step_rows // 8):
            out = out + x[j * 8:(j + 1) * 8]
        return out

    zero = jnp.zeros((8, TOK), F32)

    def student(i, carry):
        at = pl.ds(pl.multiple_of(i * step_rows, step_rows), step_rows)
        logit = ls[at, :]
        pupil = 30.0 * jnp.tanh(logit / 30.0)
        e = jnp.exp(pupil - 30.0)
        slope = 1.0 - (pupil / 30.0) ** 2
        pu[at, :], ep[at, :], qq[at, :] = pupil, e, slope
        sl = slope * logit
        ql[at, :] = sl
        return carry[0] + fold(e), carry[1] + fold(e * sl)

    zs8, u8 = lax.fori_loop(0, VOC // step_rows, student, (zero, zero))

    last(1)
    all_from_sibling(1)

    def teacher_dot(i, _):
        b = xt[pl.ds(i * N, N)].reshape(N * TF, TOK)
        lt[...] += dot(wtt[i], b)
        return 0

    lt[...] = jnp.zeros_like(lt)
    lax.fori_loop(0, 4, teacher_dot, 0)

    def teacher(i, carry):
        at = pl.ds(pl.multiple_of(i * step_rows, step_rows), step_rows)
        teach = 30.0 * jnp.tanh(lt[at, :] / 30.0)
        e = jnp.exp(teach - 30.0)
        et[at, :] = e
        return (
            carry[0] + fold(e),
            carry[1] + fold(e * (teach - pu[at, :])),
            carry[2] + fold(e * ql[at, :]),
        )

    zt8, c8, v8 = lax.fori_loop(0, VOC // step_rows, teacher, (zero, zero, zero))
    five = [jnp.sum(t, axis=0, keepdims=True) for t in (zt8, zs8, c8, u8, v8)]
    s_own[...] = jnp.concatenate(five + [jnp.zeros((3, TOK), F32)], axis=0)

    push_sums = remote(s_own, s_sib, a_send.at[0], a_recv.at[0], sibling)
    push_sums.start()
    push_sums.wait_recv()
    sent.append(push_sums)
    value = s_own[...] + s_sib[...]

    def line(buf, send, recv, here, who, value):
        buf[here] = value
        for j in range(1, N):
            copy = remote(buf.at[here], buf.at[here], send.at[j], recv.at[j], who((here + j) % N))
            copy.start()
            sent.append(copy)
        for j in range(1, N):
            at = (here + N - j) % N
            remote(buf.at[at], buf.at[at], send.at[j], recv.at[j], sibling).wait_recv()
        out = buf[0]
        for j in range(1, N):
            out = out + buf[j]
        return out

    value = line(s_z, z_send, z_recv, z, lambda t: dev(xl, y, xh, t, s), value)
    value = line(s_y, y_send, y_recv, y, lambda t: dev(xl, t, xh, z, s), value)
    here = xh * 2 + xl
    s_x[here] = value
    for j, (a, b) in enumerate(((1 - xl, xh), (xl, 1 - xh), (1 - xl, 1 - xh))):
        copy = remote(s_x.at[here], s_x.at[here], x_send.at[j], x_recv.at[j], dev(a, y, b, z, s))
        copy.start()
        sent.append(copy)
    for j, (a, b) in enumerate(((1 - xl, xh), (xl, 1 - xh), (1 - xl, 1 - xh))):
        at = b * 2 + a
        remote(s_x.at[at], s_x.at[at], x_send.at[j], x_recv.at[j], sibling).wait_recv()
    value = s_x[0] + s_x[1] + s_x[2] + s_x[3]
    zt, zs, cross, us, vs = (value[i:i + 1] for i in range(5))

    maskf = mask[...].astype(F32)
    weight = maskf / jnp.maximum(jnp.sum(maskf, axis=1, keepdims=True), 1.0)
    token_kl = cross / zt - jnp.log(zt) + jnp.log(zs)
    over_s, over_t = weight / zs, weight / zt

    def gradient(i, _):
        at = pl.ds(pl.multiple_of(i * step_rows, step_rows), step_rows)
        dpu[at, :] = ((ep[at, :] * over_s - et[at, :] * over_t) * qq[at, :]).astype(BF16)
        return 0

    lax.fori_loop(0, VOC // step_rows, gradient, 0)

    offsets = (4, 3, -3, 2, -2, 1, -1, 0)
    for i, off in enumerate(offsets):
        theirs = (1 - s) * N + (q + off + N) % N
        g_out[i] = dot(wsr[theirs], dpu[...]).astype(BF16)
        copy = remote(g_out.at[i], g_in.at[i], gs_send.at[i], gs_recv.at[i], sibling)
        copy.start()
        sent.append(copy)
        g_own[i] = dot(wsr[s * N + (p + off + N) % N], dpu[...])

    kl_out[...] = token_kl
    loss_out[...] = jnp.sum(weight * token_kl, axis=1, keepdims=True)
    rowdot = (us * over_s - vs * over_t) / scale
    stacked = jnp.concatenate([scale, rowdot, jnp.zeros((126, TOK), F32)], axis=0)
    cols[...] = stacked.T

    def own(i):
        remote(g_out.at[i], g_in.at[i], gs_send.at[i], gs_recv.at[i], sibling).wait_recv()
        return g_own[i] + g_in[i].astype(F32)

    cut = (0, SP), (SP, 2 * SF)

    def hop(way, step, whole, value):
        i = way * 4 + step
        lo, hi = (0, 2 * SF) if whole else cut[way]
        r_out[i, lo:hi, :] = value.astype(BF16)
        copy = remote(
            r_out.at[i, lo:hi], r_in.at[i, lo:hi], rr_send.at[i], rr_recv.at[i], (right, left)[way]
        )
        copy.start()
        sent.append(copy)

    def arrive(way, step, whole):
        i = way * 4 + step
        lo, hi = (0, 2 * SF) if whole else cut[way]
        remote(
            r_out.at[i, lo:hi], r_in.at[i, lo:hi], rr_send.at[i], rr_recv.at[i], sibling
        ).wait_recv()
        return r_in[i, lo:hi, :].astype(F32)

    mine = own(0)
    hop(0, 0, False, mine[:SP])
    hop(1, 0, False, mine[SP:])
    mine = own(1)
    hop(0, 1, True, jnp.concatenate([mine[:SP] + arrive(0, 0, False), mine[SP:]], axis=0))
    mine = own(2)
    hop(1, 1, True, jnp.concatenate([mine[:SP], mine[SP:] + arrive(1, 0, False)], axis=0))
    for step in (2, 3):
        for way in (0, 1):
            mine = own(2 * step - 1 + way)
            hop(way, step, True, mine + arrive(way, step - 1, True))
    mine = own(7)
    g_own[0] = mine + arrive(0, 3, True) + arrive(1, 3, True)

    give = g_own[0, pl.ds(pl.multiple_of((1 - xh) * SF, 8), SF), :]
    e_out[...] = jnp.concatenate([give, jnp.zeros((SP - SF, TOK), F32)], axis=0).astype(BF16)
    copy = remote(e_out, e_in, e_send.at[0], e_recv.at[0], across)
    copy.start()
    sent.append(copy)
    keep = g_own[0, pl.ds(pl.multiple_of(xh * SF, 8), SF), :]
    x_held = xs[mine_s].astype(F32)[:SF] * scale
    gains = gb[pl.ds(pl.multiple_of(v * SF, 8), SF), :]
    filler = jnp.zeros((128 - SF, 128), F32)
    gain_row = jnp.concatenate([gains, filler], axis=0).T[:ROWS]
    mycols = cols[pl.ds(pl.multiple_of(d * ROWS, 8), ROWS), :]
    my_scale, my_rowdot = mycols[:, 0:1], mycols[:, 1:2]
    copy.wait_recv()
    keep = keep + e_in[...].astype(F32)[:SF]
    gain_grad = jnp.sum(keep * x_held, axis=1, keepdims=True)
    gain_grad = jnp.concatenate([jnp.broadcast_to(gain_grad, (SF, 128)), filler], axis=0).T[:8]
    rough = gain_grad.astype(BF16).astype(F32)
    row = lax.broadcasted_iota(jnp.int32, (8, 128), 0)
    gain_grad = jnp.where(row == 0, rough, gain_grad - rough)
    keep = jnp.concatenate([keep, jnp.zeros((128 - SF, TOK), F32)], axis=0).T
    for m in range(2 * N):
        f_out[m] = jnp.concatenate([keep[m * ROWS:(m + 1) * ROWS], gain_grad], axis=0).astype(BF16)
    slot = xl * N + q

    def final_send(m):
        return remote(f_out.at[m], f_in.at[slot], f_send.at[m], f_recv.at[slot], owner(m))

    def is_other(m):
        who = owner(m)
        return jnp.logical_not(jnp.logical_and(who[0] == d, who[1] == v))

    def send_final(i, _):
        m = (d + 1 + i) % (2 * N)

        @pl.when(is_other(m))
        def _():
            final_send(m).start()

        return 0

    lax.fori_loop(0, 2 * N, send_final, 0)

    @pl.when(self_in)
    def _():
        f_in[slot] = f_out[d]

    def wait_final(m, _):
        @pl.when(jnp.logical_not(jnp.logical_and(self_in, m == slot)))
        def _():
            remote(f_out.at[m], f_in.at[m], f_send.at[m], f_recv.at[m], sibling).wait_recv()

        return 0

    lax.fori_loop(0, 2 * N, wait_final, 0)
    got_all = f_in[0].astype(F32)
    for m in range(1, 2 * N):
        got_all = got_all + f_in[m].astype(F32)
    dnormed = got_all[:ROWS]
    x = pad_s[...]
    grad = gain_row * dnormed * my_scale - x * (my_scale**3 * my_rowdot / (SF * 4 * N))
    gh_out[...] = grad[:, :SF]
    gg_out[...] = (got_all[ROWS:ROWS + 1] + got_all[ROWS + 1:ROWS + 2])[:, :SF]

    for copy in sent:
        copy.wait_send()

    def finish(m, _):
        @pl.when(away(m))
        def _():
            piece_send(m).wait_send()

        @pl.when(is_other(m))
        def _():
            final_send(m).wait_send()

        return 0

    lax.fori_loop(0, 2 * N, finish, 0)


def on_device(teacher_hidden, teacher_head, student_hidden, student_gain, student_head, token_mask):
    def shape(*dims):
        return jax.ShapeDtypeStruct(dims, F32)

    vmem = pl.BlockSpec(memory_space=pltpu.VMEM)
    anywhere = pl.BlockSpec(memory_space=pl.ANY)

    def half(*dims):
        return pltpu.VMEM(dims, BF16)

    def full(*dims):
        return pltpu.VMEM(dims, F32)

    dma = pltpu.SemaphoreType.DMA
    kl, loss, gh, gg = pl.pallas_call(
        body,
        out_shape=(shape(1, TOK), shape(1, 1), shape(ROWS, SF), shape(1, SF)),
        in_specs=[vmem, vmem, vmem, vmem, anywhere, anywhere],
        out_specs=(vmem, vmem, vmem, vmem),
        scratch_shapes=[
            half(4608, VOC), half(2304, VOC),
            half(4, VOC, 1152), half(2, VOC, 1152), half(16, TF, VOC),
            full(2304, 128), full(ROWS, 256), full(ROWS, 128),
            half(2 * ROWS, 128), half(16, 2 * ROWS, 128),
            half(32, TF, TOK), half(32, SP, TOK), half(16, TF, TOK),
            full(VOC, TOK), full(VOC, TOK), full(VOC, TOK), full(VOC, TOK),
            full(VOC, TOK), full(VOC, TOK), full(VOC, TOK), half(VOC, TOK),
            full(8, TOK), full(8, TOK), full(N, 8, TOK), full(N, 8, TOK), full(4, 8, TOK),
            full(TOK, 128),
            full(8, TF, TOK), half(8, TF, TOK), half(8, TF, TOK),
            half(8, TF, TOK), half(8, TF, TOK),
            half(SP, TOK), half(SP, TOK),
            half(16, 32, 128), half(16, 32, 128),
            dma((2,)), dma((16,)), dma((16,)), dma((2,)), dma((2,)),
            dma((32,)), dma((32,)), dma((32,)), dma((32,)),
            dma((1,)), dma((1,)), dma((8,)), dma((8,)), dma((8,)), dma((8,)), dma((3,)), dma((3,)),
            dma((8,)), dma((8,)), dma((8,)), dma((8,)), dma((1,)), dma((1,)), dma((16,)), dma((16,)),
        ],
        compiler_params=pltpu.CompilerParams(
            collective_id=0, has_side_effects=True, vmem_limit_bytes=56 * 1024 * 1024
        ),
        name="distill",
    )(
        teacher_hidden, student_hidden, student_gain.reshape(18, 128), token_mask.reshape(1, TOK),
        teacher_head, student_head,
    )
    return kl.reshape(TOK), loss.reshape(()), gh, gg.reshape(SF)


def solution(mesh):
    placed = (
        P("dp", "vocab"),
        P(None, ("dp", "vocab")),
        P("dp", "vocab"),
        P(),
        P(None, ("dp", "vocab")),
        P(),
    )
    return jax.shard_map(
        on_device,
        mesh=mesh,
        in_specs=placed,
        out_specs=(P(), P(), P("dp", "vocab"), P("vocab")),
        check_vma=False,
    )
```

```python
import jax
import jax.numpy as jnp
from jax import lax
from jax.experimental import pallas as pl
from jax.experimental.pallas import tpu as pltpu
from jax.sharding import PartitionSpec as P

F32, BF16 = jnp.float32, jnp.bfloat16
MESH = pl.DeviceIdType.MESH
N = 8
TOK, ROWS = 384, 24
TF, SF = 144, 72
SP = 80
VOC = 256
STOP = 99


def body(
    th, sh, gain, mask, wt_hbm, ws_hbm,
    kl_out, loss_out, gh_out, gg_out,
    wt, ws, wtt, wst0, wst1, wsr, gb, grow, perm, pad_t, pad_s, piece, got, xt, xs, ns0, ns1, sq, scol,
    ls, lt, pu, ep, qq, ql, et, dpu, s_own, s_sib, s_z, s_y, s_x, d_own, d_sib, d_z, d_y, d_x, cols, xturn, held,
    g_own, g_out, g_in, r_out, r_in, e_out, e_in, f_out, f_in,
    w_sem, p_send, p_recv, h_send, h_recv, ring_send, ring_recv, sib_send, sib_recv,
    a_send, a_recv, z_send, z_recv, y_send, y_recv, x_send, x_recv,
    gs_send, gs_recv, rr_send, rr_recv, e_send, e_recv, f_send, f_recv,
):
    d, v = lax.axis_index("dp"), lax.axis_index("vocab")
    xl, y = d // N, d % N
    s, z, xh = v % 2, (v // 2) % N, v // (2 * N)
    first = s == 0
    p = jnp.where(first, z, y)
    q = jnp.where(first, y, z)

    def dev(xl, y, xh, z, s):
        return (xl * N + y, (xh * N + z) * 2 + s)

    def ring(place):
        return dev(xl, jnp.where(first, y, place), xh, jnp.where(first, place, z), s)

    def group(m):
        j = m % N
        return dev(m // N, jnp.where(first, j, y), xh, jnp.where(first, z, j), s)

    def owner(m):
        return dev(m // N, m % N, xh, p, s)

    slot = xl * N + q
    self_in = jnp.logical_or(first, y == z)
    right, left = ring((p + 1) % N), ring((p + N - 1) % N)
    sibling = dev(xl, y, xh, z, 1 - s)
    across = dev(1 - xl, y, 1 - xh, z, s)

    def remote(src, dst, send, recv, to):
        return pltpu.make_async_remote_copy(
            src_ref=src, dst_ref=dst, send_sem=send, recv_sem=recv, device_id=to, device_id_type=MESH
        )

    wt_copy = pltpu.make_async_copy(wt_hbm, wt, w_sem.at[0])
    ws_copy = pltpu.make_async_copy(ws_hbm, ws, w_sem.at[1])
    wt_copy.start()
    ws_copy.start()

    barrier = pltpu.get_barrier_semaphore()

    def tell(to):
        pl.semaphore_signal(barrier, inc=1, device_id=to, device_id_type=MESH)

    def greet(i, _):
        tell(group((slot + i) % (2 * N)))
        return 0

    for to in (right, left, sibling, across):
        tell(to)
    lax.fori_loop(1, 2 * N, greet, 0)

    pad_t[...] = jnp.zeros_like(pad_t)
    pad_s[...] = jnp.zeros_like(pad_s)
    pad_t[:, :TF] = th[...].astype(F32)
    pad_s[:, :SF] = sh[...].astype(F32)
    lane = lax.broadcasted_iota(jnp.int32, (ROWS, 128), 1)
    low = jnp.where(lane < TF - 128, pad_t[:, 128:256], pltpu.roll(pad_s[...], TF - 128, 1))
    piece[...] = jnp.concatenate([pad_t[:, :128], low], axis=0).astype(BF16)

    got[slot] = piece[...]
    pl.semaphore_wait(barrier, 2 * N - 1 + 4)

    def piece_send(m):
        return remote(piece, got.at[slot], p_send.at[m], p_recv.at[slot], group(m))

    def send_pieces(i, _):
        piece_send((slot + i) % (2 * N)).start()
        return 0

    lax.fori_loop(1, 2 * N, send_pieces, 0)

    for i in range(18):
        gb[i * 128:(i + 1) * 128, :] = jnp.broadcast_to(gain[i:i + 1, :], (128, 128)).T
    ws_copy.wait()

    def reorder(c, _):
        one = ws[pl.ds(pl.multiple_of(c * TF, 16), TF), :].astype(F32)
        two = ws[pl.ds(pl.multiple_of((N + c) * TF, 16), TF), :].astype(F32)
        wsr[c] = jnp.concatenate([one[:SF], two[:SF]], axis=0).astype(BF16)
        wsr[N + c] = jnp.concatenate([one[SF:], two[SF:]], axis=0).astype(BF16)
        return 0

    lax.fori_loop(0, N, reorder, 0)

    for j in range(9):
        block = wsr[0:N].reshape(N * TF, VOC)[j * 128:(j + 1) * 128]
        wst0[:, j * 128:(j + 1) * 128] = block.T
    for h in (0, 1):
        rows = [wsr[N + c].astype(F32)[h * SF:(h + 1) * SF] for c in range(N)]
        rows = jnp.concatenate(rows + [jnp.zeros((64, VOC), F32)], axis=0).astype(BF16)
        gains = [gb[((h * N + c) * 2 + 1) * SF:((h * N + c) * 2 + 2) * SF, :] for c in range(N)]
        gains = jnp.concatenate(gains + [jnp.zeros((64, 128), F32)], axis=0)
        for j in range(5):
            at = slice(j * 128, (j + 1) * 128)
            wst1[h, :, at] = rows[at].T
            grow[h, :, at] = gains[at].T[:8]

    at = lax.broadcasted_iota(jnp.int32, (TOK, TOK), 1)
    group_of = (at * 2731) >> 16
    token = ((group_of & 1) * N + (group_of >> 1)) * ROWS + (at - group_of * ROWS)
    perm[...] = (token == lax.broadcasted_iota(jnp.int32, (TOK, TOK), 0)).astype(F32).astype(BF16)

    def turn_teacher(i):
        core, h = i // 2, i % 2
        base = [((h * N + c) * 2 + core) * TF for c in range(N)]
        if core == 0:
            rows = jnp.concatenate([wt[b:b + TF, :] for b in base], axis=0)
            blocks = [rows[j * 128:(j + 1) * 128] for j in range(9)]
        else:
            blocks = [wt[b:b + 128, :] for b in base]
            blocks.append(jnp.concatenate([wt[b + 128:b + TF, :] for b in base], axis=0))
        for j, block in enumerate(blocks):
            wtt[i, :, j * 128:(j + 1) * 128] = block.T

    def wait_pieces(i, _):
        m = (slot + i) % (2 * N)
        remote(piece, got.at[m], p_send.at[m], p_recv.at[m], sibling).wait_recv()
        return 0

    lax.fori_loop(1, 2 * N, wait_pieces, 0)

    mine = s * 2 * N + xh * N + p
    tail = TF - 128

    @pl.when(first)
    def _():
        pieces = [got[a * N + j].astype(F32) for j in range(N) for a in (0, 1)]
        upper = jnp.concatenate([t[:ROWS] for t in pieces], axis=0).T
        lower = jnp.concatenate([t[ROWS:] for t in pieces], axis=0).T
        for c in range(3):
            at = slice(c * 128, (c + 1) * 128)
            xt[mine, c * TF:(c + 1) * TF, :] = jnp.concatenate([upper[:, at], lower[:tail, at]], axis=0).astype(BF16)
            xs[mine, c * SP:(c + 1) * SP, :] = lower[tail:tail + SP, at].astype(BF16)

    @pl.when(jnp.logical_not(first))
    def _():
        lanes = lax.broadcasted_iota(jnp.int32, (2 * ROWS, 128), 1)
        blank = jnp.zeros((2 * ROWS, 128), F32)
        rest, student = blank, [blank] * 5
        for j in range(N):
            one, two = got[j].astype(F32), got[N + j].astype(F32)
            upper = jnp.concatenate([one[:ROWS], two[:ROWS]], axis=0)
            lower = jnp.concatenate([one[ROWS:], two[ROWS:]], axis=0)
            xt[mine, j * 48:(j + 1) * 48, :] = upper.astype(BF16)
            turned = pltpu.roll(lower, tail * j, 1) if j else lower
            rest = jnp.where(jnp.logical_and(lanes >= tail * j, lanes < tail * (j + 1)), turned, rest)
            a, b = SF * j // 128, SF * j % 128
            turned = pltpu.roll(lower, (b - tail) % 128, 1) if b != tail else lower
            student[a] = jnp.where(jnp.logical_and(lanes >= b, lanes < b + SF), turned, student[a])
            if b + SF > 128:
                student[a + 1] = jnp.where(lanes < b + SF - 128, turned, student[a + 1])
        xt[mine, 8 * 48:9 * 48, :] = rest.astype(BF16)
        for c in range(5):
            xs[mine, c * 48:(c + 1) * 48, :] = student[c].astype(BF16)

    def unit(core, place, other, teacher):
        half = 1 - xh if other else xh
        i = core * 2 * N + half * N + place
        return xt.at[i] if teacher else xs.at[i]

    sent = []

    def push(ref, send, recv, to):
        copy = remote(ref, ref, send, recv, to)
        copy.start()
        sent.append(copy)

    for kind in (0, 1):
        push(unit(s, p, 0, kind), h_send.at[kind], h_recv.at[kind], across)

    units = [(0, 0), (0, 1), (1, 0), (1, 1)]

    def to_ring(way, step, u, place):
        i = (way * 4 + step) * 4 + u
        push(unit(s, place, *units[u]), ring_send.at[i], ring_recv.at[i], (right, left)[way])

    def from_ring(way, step, u, place):
        i = (way * 4 + step) * 4 + u
        ref = unit(s, place, *units[u])
        remote(ref, ref, ring_send.at[i], ring_recv.at[i], sibling).wait_recv()

    def to_sibling(slot, u, place):
        i = slot * 4 + u
        push(unit(s, place, *units[u]), sib_send.at[i], sib_recv.at[i], sibling)

    def from_sibling(slot, u, place):
        i = slot * 4 + u
        ref = unit(1 - s, place, *units[u])
        remote(ref, ref, sib_send.at[i], sib_recv.at[i], sibling).wait_recv()

    def behind(place, way, step):
        return (place + (N - step if way == 0 else step)) % N

    def from_across(kind):
        ref = unit(s, p, 1, kind)
        remote(ref, ref, h_send.at[kind], h_recv.at[kind], sibling).wait_recv()

    def start_ring(u):
        to_ring(0, 0, u, p)
        to_ring(1, 0, u, p)
        to_sibling(0, u, p)

    def go_round(step, other):
        for kind in (0, 1):
            u = units.index((other, kind))
            for way in (0, 1):
                place = behind(p, way, step)
                from_ring(way, step - 1, u, place)
                if step < 3 or other == way:
                    to_ring(way, step, u, place)
                to_sibling(way * 3 + step, u, place)

    start_ring(0)
    start_ring(1)
    wt_copy.wait()
    turn_teacher(0)
    go_round(1, 0)
    from_across(0)
    start_ring(2)
    from_across(1)
    start_ring(3)
    turn_teacher(1)
    go_round(2, 0)
    go_round(1, 1)
    turn_teacher(2)
    go_round(3, 0)
    go_round(2, 1)
    turn_teacher(3)
    go_round(3, 1)

    far, sib_far = behind(p, 0, 4), behind(q, 0, 4)

    def last(kind):
        for way in (0, 1):
            u = units.index((way, kind))
            from_ring(way, 3, u, far)
            to_sibling(7, u, far)

    def all_from_sibling(kind):
        for other in (0, 1):
            u = units.index((other, kind))
            from_sibling(0, u, q)
            for step in (1, 2, 3):
                for way in (0, 1):
                    from_sibling(way * 3 + step, u, behind(q, way, step))
            from_sibling(7, u, sib_far)

    last(0)
    all_from_sibling(0)

    def squares(i, total):
        parts = []
        for c in range(3):
            x = xs[i, c * SP:(c + 1) * SP, :].astype(F32)
            part = x[0:8] * x[0:8]
            for j in range(1, SF // 8):
                part = part + x[j * 8:(j + 1) * 8] * x[j * 8:(j + 1) * 8]
            parts.append(part)
        return total + jnp.concatenate(parts, axis=1)

    def squares_rows(j, _):
        part = jnp.zeros((48, 128), F32)
        for h in (0, 1):
            for c in range(5):
                x = xs[2 * N + h * N + j, c * 48:(c + 1) * 48, :].astype(F32)
                part = part + x * x
        sq[pl.ds(pl.multiple_of(j * 48, 48), 48), :] = part
        return 0

    total = lax.fori_loop(0, 2 * N, squares, jnp.zeros((8, TOK), F32))
    lax.fori_loop(0, N, squares_rows, 0)
    total = jnp.sum(total, axis=0, keepdims=True) + jnp.sum(sq[...].T, axis=0, keepdims=True)
    scale = lax.rsqrt(total / (SF * 4 * N) + 1e-6)
    scol[...] = jnp.broadcast_to(scale, (128, TOK)).T

    def features_first(i):
        x = xs[i].astype(F32)
        return jnp.concatenate([x[c * SP:c * SP + SF] for c in range(3)], axis=1)

    def normalise(c, _):
        for half in (0, 1):
            at = pl.multiple_of((half * N + c) * 2 * SF, 8)
            g = gb[pl.ds(at, SF), :]
            n = (features_first(half * N + c) * scale) * jnp.concatenate([g, g, g], axis=1)
            if half == 0:
                head = n
        ns0[c] = jnp.concatenate([head, n], axis=0).astype(BF16)
        return 0

    def normalise_rows(j, _):
        at = pl.ds(pl.multiple_of(j * 48, 48), 48)
        sc = scol[at, :]
        for h in (0, 1):
            for c in range(5):
                x = xs[2 * N + h * N + j, c * 48:(c + 1) * 48, :].astype(F32)
                n = (x * sc) * grow[h, 0:1, c * 128:(c + 1) * 128]
                ns1[h, at, c * 128:(c + 1) * 128] = n.astype(BF16)
        return 0

    lax.fori_loop(0, N, normalise, 0)
    lax.fori_loop(0, N, normalise_rows, 0)

    def dot(a, b):
        return jnp.dot(a, b, preferred_element_type=F32)

    def dot_rows(a, b):
        return lax.dot_general(a, b, (((1,), (1,)), ((), ())), preferred_element_type=F32)

    ls[...] = dot(wst0[...], ns0[...].reshape(N * TF, TOK))
    ls[...] += dot_rows(wst1[0], ns1[0])
    ls[...] += dot_rows(wst1[1], ns1[1])

    step_rows = 32

    def fold(x):
        out = x[0:8]
        for j in range(1, step_rows // 8):
            out = out + x[j * 8:(j + 1) * 8]
        return out

    zero = jnp.zeros((8, TOK), F32)

    def student(i, carry):
        at = pl.ds(pl.multiple_of(i * step_rows, step_rows), step_rows)
        logit = ls[at, :]
        pupil = 30.0 * jnp.tanh(logit / 30.0)
        e = jnp.exp(pupil - 30.0)
        slope = 1.0 - (pupil / 30.0) ** 2
        pu[at, :], ep[at, :], qq[at, :] = pupil, e, slope
        sl = slope * logit
        ql[at, :] = sl
        return carry[0] + fold(e), carry[1] + fold(e * sl)

    zs8, u8 = lax.fori_loop(0, VOC // step_rows, student, (zero, zero))

    last(1)
    all_from_sibling(1)

    def tokens_last(h):
        cs = [xt[h * N:(h + 1) * N, c * TF:(c + 1) * TF, :].reshape(N * TF, 128) for c in range(3)]
        return jnp.concatenate(cs, axis=1)

    def tokens_first(h):
        at = 2 * N + h * N
        cs = [xt[at:at + N, c * 48:(c + 1) * 48, :].reshape(TOK, 128) for c in range(9)]
        return jnp.concatenate(cs, axis=1)

    lt[...] = dot(wtt[0], tokens_last(0))
    lt[...] += dot(wtt[1], tokens_last(1))
    lt[...] += dot_rows(wtt[2], tokens_first(0))
    lt[...] += dot_rows(wtt[3], tokens_first(1))

    def teacher(i, carry):
        at = pl.ds(pl.multiple_of(i * step_rows, step_rows), step_rows)
        teach = 30.0 * jnp.tanh(lt[at, :] / 30.0)
        e = jnp.exp(teach - 30.0)
        et[at, :] = e
        return (
            carry[0] + fold(e),
            carry[1] + fold(e * (teach - pu[at, :])),
            carry[2] + fold(e * ql[at, :]),
        )

    zt8, c8, v8 = lax.fori_loop(0, VOC // step_rows, teacher, (zero, zero, zero))
    fold8 = [jnp.sum(t, axis=0, keepdims=True) for t in (zt8, zs8, c8, u8, v8)]
    s_own[...] = jnp.concatenate(fold8[:3] + [jnp.zeros((1, TOK), F32)], axis=0)
    d_own[...] = jnp.concatenate(fold8[3:], axis=0)

    def core_start(own, sib, k):
        copy = remote(own, sib, a_send.at[k], a_recv.at[k], sibling)
        copy.start()
        sent.append(copy)
        return copy

    def line_start(buf, send, recv, k, here, who, value):
        buf[here] = value
        for j in range(1, N):
            i = k * N + j
            copy = remote(buf.at[here], buf.at[here], send.at[i], recv.at[i], who((here + j) % N))
            copy.start()
            sent.append(copy)

    def line_end(buf, send, recv, k, here):
        for j in range(1, N):
            i, at = k * N + j, (here + N - j) % N
            remote(buf.at[at], buf.at[at], send.at[i], recv.at[i], sibling).wait_recv()
        out = buf[0]
        for j in range(1, N):
            out = out + buf[j]
        return out

    others = ((1 - xl, xh), (xl, 1 - xh), (1 - xl, 1 - xh))

    def x_start(buf, k, value):
        here = xh * 2 + xl
        buf[here] = value
        for j, (a, b) in enumerate(others):
            i = k * 3 + j
            copy = remote(buf.at[here], buf.at[here], x_send.at[i], x_recv.at[i], dev(a, y, b, z, s))
            copy.start()
            sent.append(copy)

    def x_end(buf, k):
        for j, (a, b) in enumerate(others):
            i, at = k * 3 + j, b * 2 + a
            remote(buf.at[at], buf.at[at], x_send.at[i], x_recv.at[i], sibling).wait_recv()
        return buf[0] + buf[1] + buf[2] + buf[3]

    def along_z(t):
        return dev(xl, y, xh, t, s)

    def along_y(t):
        return dev(xl, t, xh, z, s)

    main = core_start(s_own, s_sib, 0)
    late = core_start(d_own, d_sib, 1)
    main.wait_recv()
    line_start(s_z, z_send, z_recv, 0, z, along_z, s_own[...] + s_sib[...])
    late.wait_recv()
    late_value = d_own[...] + d_sib[...]
    value = line_end(s_z, z_send, z_recv, 0, z)
    line_start(s_y, y_send, y_recv, 0, y, along_y, value)
    line_start(d_z, z_send, z_recv, 1, z, along_z, late_value)
    value = line_end(s_y, y_send, y_recv, 0, y)
    x_start(s_x, 0, value)
    late_value = line_end(d_z, z_send, z_recv, 1, z)
    line_start(d_y, y_send, y_recv, 1, y, along_y, late_value)
    value = x_end(s_x, 0)
    zt, zs, cross = (value[i:i + 1] for i in range(3))

    maskf = jnp.broadcast_to(mask[...].astype(F32).reshape(1, TOK), (16, TOK)).astype(BF16)
    maskf = dot(maskf, perm[...])[0:1]
    weight = maskf / jnp.maximum(jnp.sum(maskf, axis=1, keepdims=True), 1.0)
    token_kl = cross / zt - jnp.log(zt) + jnp.log(zs)
    over_s, over_t = weight / zs, weight / zt

    def gradient(i, _):
        at = pl.ds(pl.multiple_of(i * step_rows, step_rows), step_rows)
        dpu[at, :] = ((ep[at, :] * over_s - et[at, :] * over_t) * qq[at, :]).astype(BF16)
        return 0

    lax.fori_loop(0, VOC // step_rows, gradient, 0)

    offsets = (4, 3, -3, 2, -2, 1, -1, 0)
    w_all = dpu[...]

    def chunk(i):
        off = offsets[i]
        g_out[i] = dot(wsr[(1 - s) * N + (q + off + N) % N], w_all).astype(BF16)
        copy = remote(g_out.at[i], g_in.at[i], gs_send.at[i], gs_recv.at[i], sibling)
        copy.start()
        sent.append(copy)
        g_own[i] = dot(wsr[s * N + (p + off + N) % N], w_all)

    def own(i):
        remote(g_out.at[i], g_in.at[i], gs_send.at[i], gs_recv.at[i], sibling).wait_recv()
        g_own[i] = g_own[i] + g_in[i].astype(F32)

    parts = (0, SP), (SP, 2 * SF)

    def hop(way, step, part, i):
        at, (lo, hi) = way * 4 + step, parts[part]
        value = g_own[i, lo:hi, :]
        if step > 1 or (step == 1 and part == way):
            value = value + arrive(way, step - 1, part)
        r_out[at, lo:hi, :] = value.astype(BF16)
        copy = remote(
            r_out.at[at, lo:hi], r_in.at[at, lo:hi], rr_send.at[at * 2 + part], rr_recv.at[at * 2 + part],
            (right, left)[way],
        )
        copy.start()
        sent.append(copy)

    def arrive(way, step, part):
        at, (lo, hi) = way * 4 + step, parts[part]
        remote(
            r_out.at[at, lo:hi], r_in.at[at, lo:hi], rr_send.at[at * 2 + part], rr_recv.at[at * 2 + part], sibling
        ).wait_recv()
        return r_in[at, lo:hi, :].astype(F32)

    chunk(0)
    chunk(1)
    chunk(2)
    own(0)
    hop(0, 0, 0, 0)
    hop(1, 0, 1, 0)
    own(1)
    hop(0, 1, 1, 1)
    own(2)
    hop(1, 1, 0, 2)
    chunk(3)
    chunk(4)
    hop(0, 1, 0, 1)
    hop(1, 1, 1, 2)
    own(3)
    own(4)
    chunk(5)
    chunk(6)
    chunk(7)
    hop(0, 2, 1, 3)
    hop(1, 2, 0, 4)
    hop(0, 2, 0, 3)
    hop(1, 2, 1, 4)
    own(5)
    own(6)
    own(7)

    late_value = line_end(d_y, y_send, y_recv, 1, y)
    x_start(d_x, 1, late_value)
    loss_out[...] = jnp.sum(weight * token_kl, axis=1, keepdims=True)
    rest, split = token_kl, []
    for _ in range(3):
        split.append(rest.astype(BF16).astype(F32))
        rest = rest - split[-1]
    split = jnp.concatenate(split + [jnp.zeros((13, TOK), F32)], axis=0).astype(BF16)
    placed = dot_rows(split, perm[...])
    kl_out[...] = (placed[0:1] + placed[1:2]) + placed[2:3]

    @pl.when(first)
    def _():
        held[...] = features_first(xh * N + p) * scale

    @pl.when(jnp.logical_not(first))
    def _():
        for c in range(5):
            x = xs[pl.ds(2 * N + xh * N, N), c * 48:(c + 1) * 48, :].reshape(TOK, 128).astype(F32)
            xturn[c * 128:(c + 1) * 128, :] = x.T
        held[...] = xturn[pl.ds(pl.multiple_of(p * SF, 8), SF), :] * scale

    hop(0, 3, 1, 5)
    hop(1, 3, 0, 6)
    hop(0, 3, 0, 5)
    hop(1, 3, 1, 6)
    late_value = x_end(d_x, 1)
    rowdot = (late_value[0:1] * over_s - late_value[1:2] * over_t) / scale
    stacked = jnp.concatenate([scale, rowdot, jnp.zeros((126, TOK), F32)], axis=0)
    cols[...] = stacked.T
    for part in (0, 1):
        lo, hi = parts[part]
        g_own[0, lo:hi, :] = g_own[7, lo:hi, :] + arrive(0, 3, part) + arrive(1, 3, part)

    give = g_own[0, pl.ds(pl.multiple_of((1 - xh) * SF, 8), SF), :]
    e_out[...] = jnp.concatenate([give, jnp.zeros((SP - SF, TOK), F32)], axis=0).astype(BF16)
    copy = remote(e_out, e_in, e_send.at[0], e_recv.at[0], across)
    copy.start()
    sent.append(copy)
    keep = g_own[0, pl.ds(pl.multiple_of(xh * SF, 8), SF), :]
    x_held = held[...]
    gains = gb[pl.ds(pl.multiple_of(v * SF, 8), SF), :]
    filler = jnp.zeros((128 - SF, 128), F32)
    gain_row = jnp.concatenate([gains, filler], axis=0).T[:ROWS]
    mycols = cols[pl.ds(pl.multiple_of((y * 2 + xl) * ROWS, 8), ROWS), :]
    my_scale, my_rowdot = mycols[:, 0:1], mycols[:, 1:2]
    copy.wait_recv()
    keep = keep + e_in[...].astype(F32)[:SF]
    gain_grad = jnp.sum(keep * x_held, axis=1, keepdims=True)
    gain_grad = jnp.concatenate([jnp.broadcast_to(gain_grad, (SF, 128)), filler], axis=0).T[:8]
    rough = gain_grad.astype(BF16).astype(F32)
    row = lax.broadcasted_iota(jnp.int32, (8, 128), 0)
    gain_grad = jnp.where(row == 0, rough, gain_grad - rough)
    keep = jnp.concatenate([keep, jnp.zeros((128 - SF, TOK), F32)], axis=0).T
    for m in range(2 * N):
        at = ((m % N) * 2 + m // N) * ROWS
        f_out[m] = jnp.concatenate([keep[at:at + ROWS], gain_grad], axis=0).astype(BF16)

    def final_send(m):
        return remote(f_out.at[m], f_in.at[slot], f_send.at[m], f_recv.at[slot], owner(m))

    def is_other(m):
        who = owner(m)
        return jnp.logical_not(jnp.logical_and(who[0] == d, who[1] == v))

    def send_final(i, _):
        m = (d + 1 + i) % (2 * N)

        @pl.when(is_other(m))
        def _():
            final_send(m).start()

        return 0

    lax.fori_loop(0, 2 * N, send_final, 0)

    @pl.when(self_in)
    def _():
        f_in[slot] = f_out[d]

    def wait_final(m, _):
        @pl.when(jnp.logical_not(jnp.logical_and(self_in, m == slot)))
        def _():
            remote(f_out.at[m], f_in.at[m], f_send.at[m], f_recv.at[m], sibling).wait_recv()

        return 0

    lax.fori_loop(0, 2 * N, wait_final, 0)
    got_all = f_in[0].astype(F32)
    for m in range(1, 2 * N):
        got_all = got_all + f_in[m].astype(F32)
    dnormed = got_all[:ROWS]
    x = pad_s[...]
    grad = gain_row * dnormed * my_scale - x * (my_scale**3 * my_rowdot / (SF * 4 * N))
    gh_out[...] = grad[:, :SF]
    gg_out[...] = (got_all[ROWS:ROWS + 1] + got_all[ROWS + 1:ROWS + 2])[:, :SF]

    for copy in sent:
        copy.wait_send()

    def finish(m, _):
        @pl.when(m != slot)
        def _():
            piece_send(m).wait_send()

        @pl.when(is_other(m))
        def _():
            final_send(m).wait_send()

        return 0

    lax.fori_loop(0, 2 * N, finish, 0)


def outputs(kl, loss, gh, gg, kl_out, loss_out, gh_out, gg_out):
    kl_out[...] = kl[...].reshape(TOK)
    loss_out[...] = loss[...]
    gh_out[...] = gh[...]
    gg_out[...] = gg[...].reshape(SF)


def on_device(teacher_hidden, teacher_head, student_hidden, student_gain, student_head, token_mask):
    def shape(*dims):
        return jax.ShapeDtypeStruct(dims, F32)

    vmem = pl.BlockSpec(memory_space=pltpu.VMEM)
    anywhere = pl.BlockSpec(memory_space=pl.ANY)

    def half(*dims):
        return pltpu.VMEM(dims, BF16)

    def full(*dims):
        return pltpu.VMEM(dims, F32)

    dma = pltpu.SemaphoreType.DMA
    kl, loss, gh, gg = pl.pallas_call(
        body,
        out_shape=(shape(1, TOK), shape(1, 1), shape(ROWS, SF), shape(1, SF)),
        in_specs=[vmem, vmem, vmem, vmem, anywhere, anywhere],
        out_specs=(vmem, vmem, vmem, vmem),
        scratch_shapes=[
            half(4608, VOC), half(2304, VOC),
            half(4, VOC, 1152), half(VOC, 1152), half(2, VOC, 640), half(16, TF, VOC),
            full(2304, 128), full(2, 8, 640), half(TOK, TOK),
            full(ROWS, 256), full(ROWS, 128),
            half(2 * ROWS, 128), half(16, 2 * ROWS, 128),
            half(32, 3 * TF, 128), half(32, 3 * SP, 128),
            half(N, TF, TOK), half(2, TOK, 640), full(TOK, 128), full(TOK, 128),
            full(VOC, TOK), full(VOC, TOK), full(VOC, TOK), full(VOC, TOK),
            full(VOC, TOK), full(VOC, TOK), full(VOC, TOK), half(VOC, TOK),
            full(4, TOK), full(4, TOK), full(N, 4, TOK), full(N, 4, TOK), full(4, 4, TOK),
            full(2, TOK), full(2, TOK), full(N, 2, TOK), full(N, 2, TOK), full(4, 2, TOK),
            full(TOK, 128), full(640, TOK), full(SF, TOK),
            full(8, TF, TOK), half(8, TF, TOK), half(8, TF, TOK),
            half(8, TF, TOK), half(8, TF, TOK),
            half(SP, TOK), half(SP, TOK),
            half(16, 32, 128), half(16, 32, 128),
            dma((2,)), dma((16,)), dma((16,)), dma((2,)), dma((2,)),
            dma((32,)), dma((32,)), dma((32,)), dma((32,)),
            dma((2,)), dma((2,)), dma((16,)), dma((16,)), dma((16,)), dma((16,)), dma((6,)), dma((6,)),
            dma((8,)), dma((8,)), dma((16,)), dma((16,)), dma((1,)), dma((1,)), dma((16,)), dma((16,)),
        ],
        compiler_params=pltpu.CompilerParams(
            collective_id=0, has_side_effects=True, vmem_limit_bytes=56 * 1024 * 1024
        ),
        name="distill",
    )(
        teacher_hidden, student_hidden, student_gain.reshape(18, 128), token_mask,
        teacher_head, student_head,
    )
    kl, loss, gh, gg = pl.pallas_call(
        outputs,
        out_shape=(shape(TOK), shape(1, 1), shape(ROWS, SF), shape(SF)),
        in_specs=[vmem] * 4,
        out_specs=(vmem,) * 4,
        name="outputs",
    )(kl, loss, gh, gg)
    return kl, loss.reshape(()), gh, gg


def solution(mesh):
    placed = (
        P("dp", "vocab"),
        P(None, ("dp", "vocab")),
        P("dp", "vocab"),
        P(),
        P(None, ("dp", "vocab")),
        P(),
    )
    return jax.shard_map(
        on_device,
        mesh=mesh,
        in_specs=placed,
        out_specs=(P(), P(), P("dp", "vocab"), P("vocab")),
        check_vma=False,
    )
```

```python
import jax
import jax.numpy as jnp
from jax import lax
from jax.experimental import pallas as pl
from jax.experimental.pallas import tpu as pltpu
from jax.sharding import PartitionSpec as P

F32, BF16 = jnp.float32, jnp.bfloat16
MESH = pl.DeviceIdType.MESH
N = 8
TOK, ROWS = 384, 24
TF, SF = 144, 72
SP = 80
VOC = 256
STOP = 99


def body(
    th, sh, gain, mask, wt_hbm, ws_hbm,
    kl_out, loss_out, gh_out, gg_out,
    wt, ws, wtt, wst0, wst1, wsr, gb, grow, perm, pad_t, pad_s, piece, got, xt, xs, ns0, ns1, sq, scol,
    ls, lt, pu, ep, qq, ql, et, dpu, s_z, s_y, s_x, d_z, d_y, d_x, cols, xturn, held,
    g_own, g_out, g_in, r_out, r_in, e_out, e_in, f_out, f_in,
    w_sem, p_send, p_recv, ring_send, ring_recv, sib_send, sib_recv,
    z_send, z_recv, y_send, y_recv, x_send, x_recv,
    gs_send, gs_recv, rr_send, rr_recv, e_send, e_recv, f_send, f_recv,
):
    d, v = lax.axis_index("dp"), lax.axis_index("vocab")
    xl, y = d // N, d % N
    s, z, xh = v % 2, (v // 2) % N, v // (2 * N)
    first = s == 0
    p = jnp.where(first, z, y)
    q = jnp.where(first, y, z)

    def dev(xl, y, xh, z, s):
        return (xl * N + y, (xh * N + z) * 2 + s)

    def ring(place):
        return dev(xl, jnp.where(first, y, place), xh, jnp.where(first, place, z), s)

    def member(dh, da, dj):
        j = (q + dj) % N
        return dev(xl ^ da, jnp.where(first, j, y), xh ^ dh, jnp.where(first, z, j), s)

    def owner(m):
        return dev(m // N, m % N, xh, p, s)

    slot = xl * N + q
    far_first = (4, 3, 5, 2, 6, 1, 7)
    line_mates = [
        (dh, da, dj) for dh in (0, 1) for dj in far_first + (0,) for da in (1, 0) if dh or da or dj
    ]
    self_in = jnp.logical_or(first, y == z)
    right, left = ring((p + 1) % N), ring((p + N - 1) % N)
    sibling = dev(xl, y, xh, z, 1 - s)
    across = dev(1 - xl, y, 1 - xh, z, s)

    def remote(src, dst, send, recv, to):
        return pltpu.make_async_remote_copy(
            src_ref=src, dst_ref=dst, send_sem=send, recv_sem=recv, device_id=to, device_id_type=MESH
        )

    wt_copy = pltpu.make_async_copy(wt_hbm, wt, w_sem.at[0])
    ws_copy = pltpu.make_async_copy(ws_hbm, ws, w_sem.at[1])
    wt_copy.start()
    ws_copy.start()

    barrier = pltpu.get_barrier_semaphore()

    def tell(to):
        pl.semaphore_signal(barrier, inc=1, device_id=to, device_id_type=MESH)

    for mate in line_mates:
        tell(member(*mate))
    for to in (right, left, sibling):
        tell(to)

    pad_t[...] = jnp.zeros_like(pad_t)
    pad_s[...] = jnp.zeros_like(pad_s)
    pad_t[:, :TF] = th[...].astype(F32)
    pad_s[:, :SF] = sh[...].astype(F32)
    lane = lax.broadcasted_iota(jnp.int32, (ROWS, 128), 1)
    low = jnp.where(lane < TF - 128, pad_t[:, 128:256], pltpu.roll(pad_s[...], TF - 128, 1))
    piece[...] = jnp.concatenate([pad_t[:, :128], low], axis=0).astype(BF16)

    got[xh * 2 * N + slot] = piece[...]
    pl.semaphore_wait(barrier, len(line_mates) + 3)
    sent = []

    for i, mate in enumerate(line_mates):
        copy = remote(piece, got.at[xh * 2 * N + slot], p_send.at[i], p_recv.at[i], member(*mate))
        copy.start()
        sent.append(copy)

    def wait_pieces(half):
        for i, (dh, da, dj) in enumerate(line_mates):
            if dh == half:
                at = ((xh ^ dh) * 2 + (xl ^ da)) * N + (q + N - dj) % N
                remote(piece, got.at[at], p_send.at[i], p_recv.at[i], sibling).wait_recv()

    for i in range(18):
        gb[i * 128:(i + 1) * 128, :] = jnp.broadcast_to(gain[i:i + 1, :], (128, 128)).T
    ws_copy.wait()

    def reorder(c, _):
        one = ws[pl.ds(pl.multiple_of(c * TF, 16), TF), :].astype(F32)
        two = ws[pl.ds(pl.multiple_of((N + c) * TF, 16), TF), :].astype(F32)
        wsr[c] = jnp.concatenate([one[:SF], two[:SF]], axis=0).astype(BF16)
        wsr[N + c] = jnp.concatenate([one[SF:], two[SF:]], axis=0).astype(BF16)
        return 0

    lax.fori_loop(0, N, reorder, 0)

    for j in range(9):
        block = wsr[0:N].reshape(N * TF, VOC)[j * 128:(j + 1) * 128]
        wst0[:, j * 128:(j + 1) * 128] = block.T
    for h in (0, 1):
        rows = [wsr[N + c].astype(F32)[h * SF:(h + 1) * SF] for c in range(N)]
        rows = jnp.concatenate(rows + [jnp.zeros((64, VOC), F32)], axis=0).astype(BF16)
        gains = [gb[((h * N + c) * 2 + 1) * SF:((h * N + c) * 2 + 2) * SF, :] for c in range(N)]
        gains = jnp.concatenate(gains + [jnp.zeros((64, 128), F32)], axis=0)
        for j in range(5):
            at = slice(j * 128, (j + 1) * 128)
            wst1[h, :, at] = rows[at].T
            grow[h, :, at] = gains[at].T[:8]

    at = lax.broadcasted_iota(jnp.int32, (TOK, TOK), 1)
    group_of = (at * 2731) >> 16
    token = ((group_of & 1) * N + (group_of >> 1)) * ROWS + (at - group_of * ROWS)
    perm[...] = (token == lax.broadcasted_iota(jnp.int32, (TOK, TOK), 0)).astype(F32).astype(BF16)

    def turn_teacher(i):
        core, h = i // 2, i % 2
        base = [((h * N + c) * 2 + core) * TF for c in range(N)]
        if core == 0:
            rows = jnp.concatenate([wt[b:b + TF, :] for b in base], axis=0)
            blocks = [rows[j * 128:(j + 1) * 128] for j in range(9)]
        else:
            blocks = [wt[b:b + 128, :] for b in base]
            blocks.append(jnp.concatenate([wt[b + 128:b + TF, :] for b in base], axis=0))
        for j, block in enumerate(blocks):
            wtt[i, :, j * 128:(j + 1) * 128] = block.T

    tail = TF - 128

    def assemble(half):
        base, mine = half * 2 * N, s * 2 * N + half * N + p

        @pl.when(first)
        def _():
            pieces = [got[base + a * N + j].astype(F32) for j in range(N) for a in (0, 1)]
            upper = jnp.concatenate([t[:ROWS] for t in pieces], axis=0).T
            lower = jnp.concatenate([t[ROWS:] for t in pieces], axis=0).T
            for c in range(3):
                at = slice(c * 128, (c + 1) * 128)
                xt[mine, c * TF:(c + 1) * TF, :] = jnp.concatenate([upper[:, at], lower[:tail, at]], axis=0).astype(BF16)
                xs[mine, c * SP:(c + 1) * SP, :] = lower[tail:tail + SP, at].astype(BF16)

        @pl.when(jnp.logical_not(first))
        def _():
            lanes = lax.broadcasted_iota(jnp.int32, (2 * ROWS, 128), 1)
            blank = jnp.zeros((2 * ROWS, 128), F32)
            rest, student = blank, [blank] * 5
            for j in range(N):
                one, two = got[base + j].astype(F32), got[base + N + j].astype(F32)
                upper = jnp.concatenate([one[:ROWS], two[:ROWS]], axis=0)
                lower = jnp.concatenate([one[ROWS:], two[ROWS:]], axis=0)
                xt[mine, j * 48:(j + 1) * 48, :] = upper.astype(BF16)
                turned = pltpu.roll(lower, tail * j, 1) if j else lower
                rest = jnp.where(jnp.logical_and(lanes >= tail * j, lanes < tail * (j + 1)), turned, rest)
                a, b = SF * j // 128, SF * j % 128
                turned = pltpu.roll(lower, (b - tail) % 128, 1) if b != tail else lower
                student[a] = jnp.where(jnp.logical_and(lanes >= b, lanes < b + SF), turned, student[a])
                if b + SF > 128:
                    student[a + 1] = jnp.where(lanes < b + SF - 128, turned, student[a + 1])
            xt[mine, 8 * 48:9 * 48, :] = rest.astype(BF16)
            for c in range(5):
                xs[mine, c * 48:(c + 1) * 48, :] = student[c].astype(BF16)

    def unit(core, place, other, part):
        i = core * 2 * N + (1 - xh if other else xh) * N + place
        if part == 0:
            return xs.at[i]
        return xt.at[i] if part == 4 else xt.at[i, (part - 1) * TF:part * TF]

    def push(ref, send, recv, to):
        copy = remote(ref, ref, send, recv, to)
        copy.start()
        sent.append(copy)

    def to_ring(way, step, other, part, place):
        i = (way * 4 + step) * 8 + other * 4 + part
        push(unit(s, place, other, part), ring_send.at[i], ring_recv.at[i], (right, left)[way])

    def from_ring(way, step, other, part, place):
        i = (way * 4 + step) * 8 + other * 4 + part
        ref = unit(s, place, other, part)
        remote(ref, ref, ring_send.at[i], ring_recv.at[i], sibling).wait_recv()

    def to_sibling(slot, other, part, place):
        if part in (0, 3):
            i = slot * 4 + other * 2 + part // 3
            push(unit(s, place, other, part and 4), sib_send.at[i], sib_recv.at[i], sibling)

    def from_sibling(slot, other, kind, place):
        i = slot * 4 + other * 2 + kind
        ref = unit(1 - s, place, other, kind * 4)
        remote(ref, ref, sib_send.at[i], sib_recv.at[i], sibling).wait_recv()

    def behind(place, way, step):
        return (place + (N - step if way == 0 else step)) % N

    def start_ring(other):
        for part in range(4):
            to_ring(0, 0, other, part, p)
            to_ring(1, 0, other, part, p)
            to_sibling(0, other, part, p)

    def go_round(step, other):
        for part in range(4):
            for way in (0, 1):
                place = behind(p, way, step)
                from_ring(way, step - 1, other, part, place)
                if step < 3 or other == way:
                    to_ring(way, step, other, part, place)
                to_sibling(way * 3 + step, other, part, place)

    wait_pieces(0)
    assemble(xh)
    start_ring(0)
    wait_pieces(1)
    assemble(1 - xh)
    start_ring(1)
    wt_copy.wait()
    turn_teacher(0)
    go_round(1, 0)
    go_round(1, 1)
    turn_teacher(1)
    go_round(2, 0)
    go_round(2, 1)
    turn_teacher(2)
    go_round(3, 0)
    go_round(3, 1)
    turn_teacher(3)

    far, sib_far = behind(p, 0, 4), behind(q, 0, 4)

    def last(parts):
        for part in parts:
            for way in (0, 1):
                from_ring(way, 3, way, part, far)
                to_sibling(7, way, part, far)

    def all_from_sibling(kind):
        for other in (0, 1):
            from_sibling(0, other, kind, q)
            for step in (1, 2, 3):
                for way in (0, 1):
                    from_sibling(way * 3 + step, other, kind, behind(q, way, step))
            from_sibling(7, other, kind, sib_far)

    def dot(a, b):
        return jnp.dot(a, b, preferred_element_type=F32)

    def dot_rows(a, b):
        return lax.dot_general(a, b, (((1,), (1,)), ((), ())), preferred_element_type=F32)

    def tokens_last(h):
        cs = [xt[h * N:(h + 1) * N, c * TF:(c + 1) * TF, :].reshape(N * TF, 128) for c in range(3)]
        return jnp.concatenate(cs, axis=1)

    def tokens_first(h):
        at = 2 * N + h * N
        cs = [xt[at:at + N, c * 48:(c + 1) * 48, :].reshape(TOK, 128) for c in range(9)]
        return jnp.concatenate(cs, axis=1)

    def teacher_dots(core):
        for h in (0, 1):
            lt[...] += dot_rows(wtt[2 + h], tokens_first(h)) if core else dot(wtt[h], tokens_last(h))

    last((0, 1, 2, 3))
    lt[...] = jnp.zeros_like(lt)

    @pl.when(first)
    def _():
        teacher_dots(0)

    @pl.when(jnp.logical_not(first))
    def _():
        teacher_dots(1)

    all_from_sibling(0)

    def squares(i, total):
        parts = []
        for c in range(3):
            x = xs[i, c * SP:(c + 1) * SP, :].astype(F32)
            part = x[0:8] * x[0:8]
            for j in range(1, SF // 8):
                part = part + x[j * 8:(j + 1) * 8] * x[j * 8:(j + 1) * 8]
            parts.append(part)
        return total + jnp.concatenate(parts, axis=1)

    def squares_rows(j, _):
        part = jnp.zeros((48, 128), F32)
        for h in (0, 1):
            for c in range(5):
                x = xs[2 * N + h * N + j, c * 48:(c + 1) * 48, :].astype(F32)
                part = part + x * x
        sq[pl.ds(pl.multiple_of(j * 48, 48), 48), :] = part
        return 0

    total = lax.fori_loop(0, 2 * N, squares, jnp.zeros((8, TOK), F32))
    lax.fori_loop(0, N, squares_rows, 0)
    total = jnp.sum(total, axis=0, keepdims=True) + jnp.sum(sq[...].T, axis=0, keepdims=True)
    scale = lax.rsqrt(total / (SF * 4 * N) + 1e-6)
    scol[...] = jnp.broadcast_to(scale, (128, TOK)).T

    def features_first(i):
        x = xs[i].astype(F32)
        return jnp.concatenate([x[c * SP:c * SP + SF] for c in range(3)], axis=1)

    def normalise(c, _):
        for half in (0, 1):
            at = pl.multiple_of((half * N + c) * 2 * SF, 8)
            g = gb[pl.ds(at, SF), :]
            n = (features_first(half * N + c) * scale) * jnp.concatenate([g, g, g], axis=1)
            if half == 0:
                head = n
        ns0[c] = jnp.concatenate([head, n], axis=0).astype(BF16)
        return 0

    def normalise_rows(j, _):
        at = pl.ds(pl.multiple_of(j * 48, 48), 48)
        sc = scol[at, :]
        for h in (0, 1):
            for c in range(5):
                x = xs[2 * N + h * N + j, c * 48:(c + 1) * 48, :].astype(F32)
                n = (x * sc) * grow[h, 0:1, c * 128:(c + 1) * 128]
                ns1[h, at, c * 128:(c + 1) * 128] = n.astype(BF16)
        return 0

    lax.fori_loop(0, N, normalise, 0)
    lax.fori_loop(0, N, normalise_rows, 0)

    ls[...] = dot(wst0[...], ns0[...].reshape(N * TF, TOK))
    ls[...] += dot_rows(wst1[0], ns1[0])
    ls[...] += dot_rows(wst1[1], ns1[1])

    step_rows = 32

    def fold(x):
        out = x[0:8]
        for j in range(1, step_rows // 8):
            out = out + x[j * 8:(j + 1) * 8]
        return out

    zero = jnp.zeros((8, TOK), F32)

    def student(i, carry):
        at = pl.ds(pl.multiple_of(i * step_rows, step_rows), step_rows)
        logit = ls[at, :]
        pupil = 30.0 * jnp.tanh(logit / 30.0)
        e = jnp.exp(pupil - 30.0)
        slope = 1.0 - (pupil / 30.0) ** 2
        pu[at, :], ep[at, :], qq[at, :] = pupil, e, slope
        sl = slope * logit
        ql[at, :] = sl
        return carry[0] + fold(e), carry[1] + fold(e * sl)

    zs8, u8 = lax.fori_loop(0, VOC // step_rows, student, (zero, zero))

    all_from_sibling(1)

    @pl.when(first)
    def _():
        teacher_dots(1)

    @pl.when(jnp.logical_not(first))
    def _():
        teacher_dots(0)


    def teacher(i, carry):
        at = pl.ds(pl.multiple_of(i * step_rows, step_rows), step_rows)
        teach = 30.0 * jnp.tanh(lt[at, :] / 30.0)
        e = jnp.exp(teach - 30.0)
        et[at, :] = e
        return (
            carry[0] + fold(e),
            carry[1] + fold(e * (teach - pu[at, :])),
            carry[2] + fold(e * ql[at, :]),
        )

    zt8, c8, v8 = lax.fori_loop(0, VOC // step_rows, teacher, (zero, zero, zero))
    fold8 = [jnp.sum(t, axis=0, keepdims=True) for t in (zt8, zs8, c8, u8, v8)]
    main_sums = jnp.concatenate(fold8[:2], axis=0)
    late_sums = jnp.concatenate(fold8[2:] + [jnp.zeros((1, TOK), F32)], axis=0)

    def line_start(buf, send, recv, k, here, who, value):
        buf[here] = value
        for j in far_first:
            i = k * N + j
            copy = remote(buf.at[here], buf.at[here], send.at[i], recv.at[i], who((here + j) % N))
            copy.start()
            sent.append(copy)

    def line_end(buf, send, recv, k, here):
        for j in range(1, N):
            i, at = k * N + j, (here + N - j) % N
            remote(buf.at[at], buf.at[at], send.at[i], recv.at[i], sibling).wait_recv()
        out = buf[0]
        for j in range(1, N):
            out = out + buf[j]
        return out

    others = [(dh, da, dc) for dh in (1, 0) for da in (1, 0) for dc in (0, 1) if dh or da or dc]

    def x_start(buf, k, value):
        here = (xh * 2 + xl) * 2 + s
        buf[here] = value
        for j, (dh, da, dc) in enumerate(others):
            i = k * 7 + j
            copy = remote(
                buf.at[here], buf.at[here], x_send.at[i], x_recv.at[i], dev(xl ^ da, y, xh ^ dh, z, s ^ dc)
            )
            copy.start()
            sent.append(copy)

    def x_end(buf, k):
        for j, (dh, da, dc) in enumerate(others):
            i, at = k * 7 + j, ((xh ^ dh) * 2 + (xl ^ da)) * 2 + (s ^ dc)
            remote(buf.at[at], buf.at[at], x_send.at[i], x_recv.at[i], sibling).wait_recv()
        out = buf[0]
        for j in range(1, 8):
            out = out + buf[j]
        return out

    def along_z(t):
        return dev(xl, y, xh, t, s)

    def along_y(t):
        return dev(xl, t, xh, z, s)

    line_start(s_z, z_send, z_recv, 0, z, along_z, main_sums)
    value = line_end(s_z, z_send, z_recv, 0, z)
    line_start(s_y, y_send, y_recv, 0, y, along_y, value)
    line_start(d_z, z_send, z_recv, 1, z, along_z, late_sums)
    value = line_end(s_y, y_send, y_recv, 0, y)
    x_start(s_x, 0, value)
    late_value = line_end(d_z, z_send, z_recv, 1, z)
    line_start(d_y, y_send, y_recv, 1, y, along_y, late_value)
    value = x_end(s_x, 0)
    zt, zs = value[0:1], value[1:2]

    maskf = jnp.broadcast_to(mask[...].astype(F32).reshape(1, TOK), (16, TOK)).astype(BF16)
    maskf = dot(maskf, perm[...])[0:1]
    weight = maskf / jnp.maximum(jnp.sum(maskf, axis=1, keepdims=True), 1.0)
    over_s, over_t = weight / zs, weight / zt

    def gradient(i, _):
        at = pl.ds(pl.multiple_of(i * step_rows, step_rows), step_rows)
        dpu[at, :] = ((ep[at, :] * over_s - et[at, :] * over_t) * qq[at, :]).astype(BF16)
        return 0

    lax.fori_loop(0, VOC // step_rows, gradient, 0)

    offsets = (4, 3, -3, 2, -2, 1, -1, 0)
    w_all = dpu[...]

    def chunk(i):
        off = offsets[i]
        g_out[i] = dot(wsr[(1 - s) * N + (q + off + N) % N], w_all).astype(BF16)
        copy = remote(g_out.at[i], g_in.at[i], gs_send.at[i], gs_recv.at[i], sibling)
        copy.start()
        sent.append(copy)
        g_own[i] = dot(wsr[s * N + (p + off + N) % N], w_all)

    def own(i):
        remote(g_out.at[i], g_in.at[i], gs_send.at[i], gs_recv.at[i], sibling).wait_recv()
        g_own[i] = g_own[i] + g_in[i].astype(F32)

    parts = (0, SP), (SP, 2 * SF)
    right2, left2 = ring((p + 2) % N), ring((p + N - 2) % N)

    def give(way, dist, part, i):
        at, (lo, hi) = way * 4 + dist - 1, parts[part]
        value = g_own[i, lo:hi, :]
        if dist == 2:
            value = value + take(way, 3, part)
            if part == way:
                value = value + take(way, 4, part)
        r_out[at, lo:hi, :] = value.astype(BF16)
        to = ((right, left), (right2, left2))[dist in (2, 4)][way]
        copy = remote(
            r_out.at[at, lo:hi], r_in.at[at, lo:hi], rr_send.at[at * 2 + part], rr_recv.at[at * 2 + part], to
        )
        copy.start()
        sent.append(copy)

    def take(way, dist, part):
        at, (lo, hi) = way * 4 + dist - 1, parts[part]
        remote(
            r_out.at[at, lo:hi], r_in.at[at, lo:hi], rr_send.at[at * 2 + part], rr_recv.at[at * 2 + part], sibling
        ).wait_recv()
        return r_in[at, lo:hi, :].astype(F32)

    chunk(0)
    chunk(1)
    chunk(2)
    own(0)
    give(0, 4, 0, 0)
    give(1, 4, 1, 0)
    own(1)
    give(0, 3, 1, 1)
    own(2)
    give(1, 3, 0, 2)
    give(0, 3, 0, 1)
    give(1, 3, 1, 2)
    for i in range(3, 8):
        chunk(i)
    own(5)
    own(6)
    for part in (0, 1):
        give(0, 1, part, 5)
        give(1, 1, part, 6)
    own(3)
    own(4)
    own(7)

    late_value = line_end(d_y, y_send, y_recv, 1, y)
    x_start(d_x, 1, late_value)
    @pl.when(first)
    def _():
        held[...] = features_first(xh * N + p) * scale

    @pl.when(jnp.logical_not(first))
    def _():
        for c in range(5):
            x = xs[pl.ds(2 * N + xh * N, N), c * 48:(c + 1) * 48, :].reshape(TOK, 128).astype(F32)
            xturn[c * 128:(c + 1) * 128, :] = x.T
        held[...] = xturn[pl.ds(pl.multiple_of(p * SF, 8), SF), :] * scale

    give(0, 2, 1, 3)
    give(1, 2, 0, 4)
    give(0, 2, 0, 3)
    give(1, 2, 1, 4)
    late_value = x_end(d_x, 1)
    rowdot = (late_value[1:2] * over_s - late_value[2:3] * over_t) / scale
    stacked = jnp.concatenate([scale, rowdot, jnp.zeros((126, TOK), F32)], axis=0)
    cols[...] = stacked.T
    for part in (0, 1):
        lo, hi = parts[part]
        near = g_own[7, lo:hi, :] + take(0, 1, part) + take(1, 1, part)
        g_own[0, lo:hi, :] = near + take(0, 2, part) + take(1, 2, part)

    give = g_own[0, pl.ds(pl.multiple_of((1 - xh) * SF, 8), SF), :]
    e_out[...] = jnp.concatenate([give, jnp.zeros((SP - SF, TOK), F32)], axis=0).astype(BF16)
    copy = remote(e_out, e_in, e_send.at[0], e_recv.at[0], across)
    copy.start()
    sent.append(copy)
    keep = g_own[0, pl.ds(pl.multiple_of(xh * SF, 8), SF), :]
    x_held = held[...]
    gains = gb[pl.ds(pl.multiple_of(v * SF, 8), SF), :]
    filler = jnp.zeros((128 - SF, 128), F32)
    gain_row = jnp.concatenate([gains, filler], axis=0).T[:ROWS]
    mycols = cols[pl.ds(pl.multiple_of((y * 2 + xl) * ROWS, 8), ROWS), :]
    my_scale, my_rowdot = mycols[:, 0:1], mycols[:, 1:2]
    copy.wait_recv()
    keep = keep + e_in[...].astype(F32)[:SF]
    gain_grad = jnp.sum(keep * x_held, axis=1, keepdims=True)
    gain_grad = jnp.concatenate([jnp.broadcast_to(gain_grad, (SF, 128)), filler], axis=0).T[:8]
    rough = gain_grad.astype(BF16).astype(F32)
    row = lax.broadcasted_iota(jnp.int32, (8, 128), 0)
    gain_grad = jnp.where(row == 0, rough, gain_grad - rough)
    keep = jnp.concatenate([keep, jnp.zeros((128 - SF, TOK), F32)], axis=0).T
    for m in range(2 * N):
        at = ((m % N) * 2 + m // N) * ROWS
        f_out[m] = jnp.concatenate([keep[at:at + ROWS], gain_grad], axis=0).astype(BF16)

    token_kl = late_value[0:1] / zt - jnp.log(zt) + jnp.log(zs)

    def final_send(m):
        return remote(f_out.at[m], f_in.at[slot], f_send.at[m], f_recv.at[slot], owner(m))

    def is_other(m):
        who = owner(m)
        return jnp.logical_not(jnp.logical_and(who[0] == d, who[1] == v))

    def send_final(i, _):
        m = (d + 1 + i) % (2 * N)

        @pl.when(is_other(m))
        def _():
            final_send(m).start()

        return 0

    lax.fori_loop(0, 2 * N, send_final, 0)

    loss_out[...] = jnp.sum(weight * token_kl, axis=1, keepdims=True)
    rest, split = token_kl, []
    for _ in range(3):
        split.append(rest.astype(BF16).astype(F32))
        rest = rest - split[-1]
    split = jnp.concatenate(split + [jnp.zeros((13, TOK), F32)], axis=0).astype(BF16)
    placed = dot_rows(split, perm[...])
    kl_out[...] = ((placed[0:1] + placed[1:2]) + placed[2:3]).reshape(TOK)

    @pl.when(self_in)
    def _():
        f_in[slot] = f_out[d]

    def wait_final(m, _):
        @pl.when(jnp.logical_not(jnp.logical_and(self_in, m == slot)))
        def _():
            remote(f_out.at[m], f_in.at[m], f_send.at[m], f_recv.at[m], sibling).wait_recv()

        return 0

    lax.fori_loop(0, 2 * N, wait_final, 0)
    got_all = f_in[0].astype(F32)
    for m in range(1, 2 * N):
        got_all = got_all + f_in[m].astype(F32)
    dnormed = got_all[:ROWS]
    x = pad_s[...]
    grad = gain_row * dnormed * my_scale - x * (my_scale**3 * my_rowdot / (SF * 4 * N))
    gh_out[...] = grad[:, :SF]
    gg_out[...] = (got_all[ROWS:ROWS + 1] + got_all[ROWS + 1:ROWS + 2])[:, :SF].reshape(SF)

    for copy in sent:
        copy.wait_send()

    def finish(m, _):
        @pl.when(is_other(m))
        def _():
            final_send(m).wait_send()

        return 0

    lax.fori_loop(0, 2 * N, finish, 0)


def outputs(kl, loss, gh, gg, kl_out, loss_out, gh_out, gg_out, sems):
    pairs = (kl, kl_out), (loss, loss_out), (gh, gh_out), (gg, gg_out)
    copies = [pltpu.make_async_copy(a, b, sems.at[i]) for i, (a, b) in enumerate(pairs)]
    for copy in copies:
        copy.start()
    for copy in copies:
        copy.wait()


def on_device(teacher_hidden, teacher_head, student_hidden, student_gain, student_head, token_mask):
    def shape(*dims):
        return jax.ShapeDtypeStruct(dims, F32)

    vmem = pl.BlockSpec(memory_space=pltpu.VMEM)
    anywhere = pl.BlockSpec(memory_space=pl.ANY)

    def half(*dims):
        return pltpu.VMEM(dims, BF16)

    def full(*dims):
        return pltpu.VMEM(dims, F32)

    dma = pltpu.SemaphoreType.DMA
    kl, loss, gh, gg = pl.pallas_call(
        body,
        out_shape=(shape(TOK), shape(1, 1), shape(ROWS, SF), shape(SF)),
        in_specs=[vmem, vmem, vmem, vmem, anywhere, anywhere],
        out_specs=(vmem, vmem, vmem, vmem),
        scratch_shapes=[
            half(4608, VOC), half(2304, VOC),
            half(4, VOC, 1152), half(VOC, 1152), half(2, VOC, 640), half(16, TF, VOC),
            full(2304, 128), full(2, 8, 640), half(TOK, TOK),
            full(ROWS, 256), full(ROWS, 128),
            half(2 * ROWS, 128), half(32, 2 * ROWS, 128),
            half(32, 3 * TF, 128), half(32, 3 * SP, 128),
            half(N, TF, TOK), half(2, TOK, 640), full(TOK, 128), full(TOK, 128),
            full(VOC, TOK), full(VOC, TOK), full(VOC, TOK), full(VOC, TOK),
            full(VOC, TOK), full(VOC, TOK), full(VOC, TOK), half(VOC, TOK),
            full(N, 2, TOK), full(N, 2, TOK), full(8, 2, TOK),
            full(N, 4, TOK), full(N, 4, TOK), full(8, 4, TOK),
            full(TOK, 128), full(640, TOK), full(SF, TOK),
            full(8, TF, TOK), half(8, TF, TOK), half(8, TF, TOK),
            half(8, TF, TOK), half(8, TF, TOK),
            half(SP, TOK), half(SP, TOK),
            half(16, 32, 128), half(16, 32, 128),
            dma((2,)), dma((31,)), dma((31,)),
            dma((64,)), dma((64,)), dma((32,)), dma((32,)),
            dma((16,)), dma((16,)), dma((16,)), dma((16,)), dma((14,)), dma((14,)),
            dma((8,)), dma((8,)), dma((16,)), dma((16,)), dma((1,)), dma((1,)), dma((16,)), dma((16,)),
        ],
        compiler_params=pltpu.CompilerParams(
            collective_id=0, has_side_effects=True, vmem_limit_bytes=56 * 1024 * 1024
        ),
        name="distill",
    )(
        teacher_hidden, student_hidden, student_gain.reshape(18, 128), token_mask,
        teacher_head, student_head,
    )
    kl, loss, gh, gg = pl.pallas_call(
        outputs,
        out_shape=(shape(TOK), shape(1, 1), shape(ROWS, SF), shape(SF)),
        in_specs=[anywhere] * 4,
        out_specs=(anywhere,) * 4,
        scratch_shapes=[dma((4,))],
        name="outputs",
    )(kl, loss, gh, gg)
    return kl, loss.reshape(()), gh, gg


def solution(mesh):
    placed = (
        P("dp", "vocab"),
        P(None, ("dp", "vocab")),
        P("dp", "vocab"),
        P(),
        P(None, ("dp", "vocab")),
        P(),
    )
    return jax.shard_map(
        on_device,
        mesh=mesh,
        in_specs=placed,
        out_specs=(P(), P(), P("dp", "vocab"), P("vocab")),
        check_vma=False,
    )
```

```python
import jax
import jax.numpy as jnp
from jax import lax
from jax.experimental import pallas as pl
from jax.experimental.pallas import tpu as pltpu
from jax.sharding import PartitionSpec as P

F32, BF16 = jnp.float32, jnp.bfloat16
MESH = pl.DeviceIdType.MESH
N = 8
TOK, ROWS = 384, 24
TF, SF = 144, 72
SP = 80
VOC = 256
STOP = 99


def body(
    th, sh, gain, mask, wt_hbm, ws_hbm,
    kl_out, loss_out, gh_out, gg_out,
    wt, ws, wtt, wst0, wst1, wsr, gb, grow, perm, pad_t, pad_s, piece, got, xt, xs, ns0, ns1, sq, scol,
    ls, lt, pu, ep, qq, ql, et, dpu, s_z, s_y, s_x, d_z, d_y, d_x, cols, xturn, held,
    g_own, g_out, g_in, r_out, r_in, e_out, e_in, f_out, f_in,
    w_sem, p_send, p_recv, ring_send, ring_recv, sib_send, sib_recv,
    z_send, z_recv, y_send, y_recv, x_send, x_recv,
    gs_send, gs_recv, rr_send, rr_recv, e_send, e_recv, f_send, f_recv,
):
    d, v = lax.axis_index("dp"), lax.axis_index("vocab")
    xl, y = d // N, d % N
    s, z, xh = v % 2, (v // 2) % N, v // (2 * N)
    first = s == 0
    p = jnp.where(first, z, y)
    q = jnp.where(first, y, z)

    def dev(xl, y, xh, z, s):
        return (xl * N + y, (xh * N + z) * 2 + s)

    def ring(place):
        return dev(xl, jnp.where(first, y, place), xh, jnp.where(first, place, z), s)

    def member(dh, da, dj):
        j = (q + dj) % N
        return dev(xl ^ da, jnp.where(first, j, y), xh ^ dh, jnp.where(first, z, j), s)

    def owner(m):
        return dev(m // N, m % N, xh, p, s)

    slot = xl * N + q
    far_first = (4, 3, 5, 2, 6, 1, 7)
    line_mates = [
        (dh, da, dj) for dh in (0, 1) for dj in far_first + (0,) for da in (1, 0) if dh or da or dj
    ]
    self_in = jnp.logical_or(first, y == z)
    right, left = ring((p + 1) % N), ring((p + N - 1) % N)
    sibling = dev(xl, y, xh, z, 1 - s)
    across = dev(1 - xl, y, 1 - xh, z, s)

    def remote(src, dst, send, recv, to):
        return pltpu.make_async_remote_copy(
            src_ref=src, dst_ref=dst, send_sem=send, recv_sem=recv, device_id=to, device_id_type=MESH
        )

    wt_copy = pltpu.make_async_copy(wt_hbm, wt, w_sem.at[0])
    ws_copy = pltpu.make_async_copy(ws_hbm, ws, w_sem.at[1])
    wt_copy.start()
    ws_copy.start()

    barrier = pltpu.get_barrier_semaphore()

    def tell(to):
        pl.semaphore_signal(barrier, inc=1, device_id=to, device_id_type=MESH)

    for mate in line_mates:
        tell(member(*mate))
    for to in (right, left, sibling):
        tell(to)

    pad_t[...] = jnp.zeros_like(pad_t)
    pad_s[...] = jnp.zeros_like(pad_s)
    pad_t[:, :TF] = th[...].astype(F32)
    pad_s[:, :SF] = sh[...].astype(F32)
    lane = lax.broadcasted_iota(jnp.int32, (ROWS, 128), 1)
    low = jnp.where(lane < TF - 128, pad_t[:, 128:256], pltpu.roll(pad_s[...], TF - 128, 1))
    piece[...] = jnp.concatenate([pad_t[:, :128], low], axis=0).astype(BF16)

    got[xh * 2 * N + slot] = piece[...]
    pl.semaphore_wait(barrier, len(line_mates) + 3)
    sent = []

    for i, mate in enumerate(line_mates):
        copy = remote(piece, got.at[xh * 2 * N + slot], p_send.at[i], p_recv.at[i], member(*mate))
        copy.start()
        sent.append(copy)

    def wait_pieces(half):
        for i, (dh, da, dj) in enumerate(line_mates):
            if dh == half:
                at = ((xh ^ dh) * 2 + (xl ^ da)) * N + (q + N - dj) % N
                remote(piece, got.at[at], p_send.at[i], p_recv.at[i], sibling).wait_recv()

    for i in range(18):
        gb[i * 128:(i + 1) * 128, :] = jnp.broadcast_to(gain[i:i + 1, :], (128, 128)).T
    ws_copy.wait()

    def reorder(c, _):
        one = ws[pl.ds(pl.multiple_of(c * TF, 16), TF), :].astype(F32)
        two = ws[pl.ds(pl.multiple_of((N + c) * TF, 16), TF), :].astype(F32)
        wsr[c] = jnp.concatenate([one[:SF], two[:SF]], axis=0).astype(BF16)
        wsr[N + c] = jnp.concatenate([one[SF:], two[SF:]], axis=0).astype(BF16)
        return 0

    lax.fori_loop(0, N, reorder, 0)

    for j in range(9):
        block = wsr[0:N].reshape(N * TF, VOC)[j * 128:(j + 1) * 128]
        wst0[:, j * 128:(j + 1) * 128] = block.T
    for h in (0, 1):
        rows = [wsr[N + c].astype(F32)[h * SF:(h + 1) * SF] for c in range(N)]
        rows = jnp.concatenate(rows + [jnp.zeros((64, VOC), F32)], axis=0).astype(BF16)
        gains = [gb[((h * N + c) * 2 + 1) * SF:((h * N + c) * 2 + 2) * SF, :] for c in range(N)]
        gains = jnp.concatenate(gains + [jnp.zeros((64, 128), F32)], axis=0)
        for j in range(5):
            at = slice(j * 128, (j + 1) * 128)
            wst1[h, :, at] = rows[at].T
            grow[h, :, at] = gains[at].T[:8]

    at = lax.broadcasted_iota(jnp.int32, (TOK, TOK), 1)
    group_of = (at * 2731) >> 16
    token = ((group_of & 1) * N + (group_of >> 1)) * ROWS + (at - group_of * ROWS)
    perm[...] = (token == lax.broadcasted_iota(jnp.int32, (TOK, TOK), 0)).astype(F32).astype(BF16)

    def turn_teacher(i):
        core, h = i // 2, i % 2
        base = [((h * N + c) * 2 + core) * TF for c in range(N)]
        if core == 0:
            rows = jnp.concatenate([wt[b:b + TF, :] for b in base], axis=0)
            blocks = [rows[j * 128:(j + 1) * 128] for j in range(9)]
        else:
            blocks = [wt[b:b + 128, :] for b in base]
            blocks.append(jnp.concatenate([wt[b + 128:b + TF, :] for b in base], axis=0))
        for j, block in enumerate(blocks):
            wtt[i, :, j * 128:(j + 1) * 128] = block.T

    tail = TF - 128

    def assemble(half):
        base, mine = half * 2 * N, s * 2 * N + half * N + p

        @pl.when(first)
        def _():
            pieces = [got[base + a * N + j].astype(F32) for j in range(N) for a in (0, 1)]
            upper = jnp.concatenate([t[:ROWS] for t in pieces], axis=0).T
            lower = jnp.concatenate([t[ROWS:] for t in pieces], axis=0).T
            for c in range(3):
                at = slice(c * 128, (c + 1) * 128)
                xt[mine, c * TF:(c + 1) * TF, :] = jnp.concatenate([upper[:, at], lower[:tail, at]], axis=0).astype(BF16)
                xs[mine, c * SP:(c + 1) * SP, :] = lower[tail:tail + SP, at].astype(BF16)

        @pl.when(jnp.logical_not(first))
        def _():
            lanes = lax.broadcasted_iota(jnp.int32, (2 * ROWS, 128), 1)
            blank = jnp.zeros((2 * ROWS, 128), F32)
            rest, student = blank, [blank] * 5
            for j in range(N):
                one, two = got[base + j].astype(F32), got[base + N + j].astype(F32)
                upper = jnp.concatenate([one[:ROWS], two[:ROWS]], axis=0)
                lower = jnp.concatenate([one[ROWS:], two[ROWS:]], axis=0)
                xt[mine, j * 48:(j + 1) * 48, :] = upper.astype(BF16)
                turned = pltpu.roll(lower, tail * j, 1) if j else lower
                rest = jnp.where(jnp.logical_and(lanes >= tail * j, lanes < tail * (j + 1)), turned, rest)
                a, b = SF * j // 128, SF * j % 128
                turned = pltpu.roll(lower, (b - tail) % 128, 1) if b != tail else lower
                student[a] = jnp.where(jnp.logical_and(lanes >= b, lanes < b + SF), turned, student[a])
                if b + SF > 128:
                    student[a + 1] = jnp.where(lanes < b + SF - 128, turned, student[a + 1])
            xt[mine, 8 * 48:9 * 48, :] = rest.astype(BF16)
            for c in range(5):
                xs[mine, c * 48:(c + 1) * 48, :] = student[c].astype(BF16)

    def unit(core, place, other, part):
        i = core * 2 * N + (1 - xh if other else xh) * N + place
        if part == 0:
            return xs.at[i]
        return xt.at[i] if part == 4 else xt.at[i, (part - 1) * TF:part * TF]

    def push(ref, send, recv, to):
        copy = remote(ref, ref, send, recv, to)
        copy.start()
        sent.append(copy)

    def to_ring(way, step, other, part, place):
        i = (way * 4 + step) * 8 + other * 4 + part
        push(unit(s, place, other, part), ring_send.at[i], ring_recv.at[i], (right, left)[way])

    def from_ring(way, step, other, part, place):
        i = (way * 4 + step) * 8 + other * 4 + part
        ref = unit(s, place, other, part)
        remote(ref, ref, ring_send.at[i], ring_recv.at[i], sibling).wait_recv()

    def to_sibling(slot, other, part, place):
        if part in (0, 3):
            i = slot * 4 + other * 2 + part // 3
            push(unit(s, place, other, part and 4), sib_send.at[i], sib_recv.at[i], sibling)

    def from_sibling(slot, other, kind, place):
        i = slot * 4 + other * 2 + kind
        ref = unit(1 - s, place, other, kind * 4)
        remote(ref, ref, sib_send.at[i], sib_recv.at[i], sibling).wait_recv()

    def behind(place, way, step):
        return (place + (N - step if way == 0 else step)) % N

    def start_ring(other):
        for part in range(4):
            to_ring(0, 0, other, part, p)
            to_ring(1, 0, other, part, p)
            to_sibling(0, other, part, p)

    def go_round(step, other):
        for part in range(4):
            for way in (0, 1):
                place = behind(p, way, step)
                from_ring(way, step - 1, other, part, place)
                if step < 3 or other == way:
                    to_ring(way, step, other, part, place)
                to_sibling(way * 3 + step, other, part, place)

    wait_pieces(0)
    assemble(xh)
    start_ring(0)
    wait_pieces(1)
    assemble(1 - xh)
    start_ring(1)
    wt_copy.wait()
    turn_teacher(0)
    go_round(1, 0)
    go_round(1, 1)
    turn_teacher(1)
    go_round(2, 0)
    go_round(2, 1)
    turn_teacher(2)
    go_round(3, 0)
    go_round(3, 1)
    turn_teacher(3)

    far, sib_far = behind(p, 0, 4), behind(q, 0, 4)

    def last(parts):
        for part in parts:
            for way in (0, 1):
                from_ring(way, 3, way, part, far)
                to_sibling(7, way, part, far)

    def all_from_sibling(kind):
        for other in (0, 1):
            from_sibling(0, other, kind, q)
            for step in (1, 2, 3):
                for way in (0, 1):
                    from_sibling(way * 3 + step, other, kind, behind(q, way, step))
            from_sibling(7, other, kind, sib_far)

    def dot(a, b):
        return jnp.dot(a, b, preferred_element_type=F32)

    def dot_rows(a, b):
        return lax.dot_general(a, b, (((1,), (1,)), ((), ())), preferred_element_type=F32)

    def tokens_last(h):
        cs = [xt[h * N:(h + 1) * N, c * TF:(c + 1) * TF, :].reshape(N * TF, 128) for c in range(3)]
        return jnp.concatenate(cs, axis=1)

    def tokens_first(h):
        at = 2 * N + h * N
        cs = [xt[at:at + N, c * 48:(c + 1) * 48, :].reshape(TOK, 128) for c in range(9)]
        return jnp.concatenate(cs, axis=1)

    def teacher_dots(core):
        for h in (0, 1):
            lt[...] += dot_rows(wtt[2 + h], tokens_first(h)) if core else dot(wtt[h], tokens_last(h))

    last((0, 1, 2, 3))
    lt[...] = jnp.zeros_like(lt)

    @pl.when(first)
    def _():
        teacher_dots(0)

    @pl.when(jnp.logical_not(first))
    def _():
        teacher_dots(1)

    all_from_sibling(0)

    def squares(i, total):
        parts = []
        for c in range(3):
            x = xs[i, c * SP:(c + 1) * SP, :].astype(F32)
            part = x[0:8] * x[0:8]
            for j in range(1, SF // 8):
                part = part + x[j * 8:(j + 1) * 8] * x[j * 8:(j + 1) * 8]
            parts.append(part)
        return total + jnp.concatenate(parts, axis=1)

    def squares_rows(j, _):
        part = jnp.zeros((48, 128), F32)
        for h in (0, 1):
            for c in range(5):
                x = xs[2 * N + h * N + j, c * 48:(c + 1) * 48, :].astype(F32)
                part = part + x * x
        sq[pl.ds(pl.multiple_of(j * 48, 48), 48), :] = part
        return 0

    total = lax.fori_loop(0, 2 * N, squares, jnp.zeros((8, TOK), F32))
    lax.fori_loop(0, N, squares_rows, 0)
    total = jnp.sum(total, axis=0, keepdims=True) + jnp.sum(sq[...].T, axis=0, keepdims=True)
    scale = lax.rsqrt(total / (SF * 4 * N) + 1e-6)
    scol[...] = jnp.broadcast_to(scale, (128, TOK)).T

    def features_first(i):
        x = xs[i].astype(F32)
        return jnp.concatenate([x[c * SP:c * SP + SF] for c in range(3)], axis=1)

    def normalise(c, _):
        for half in (0, 1):
            at = pl.multiple_of((half * N + c) * 2 * SF, 8)
            g = gb[pl.ds(at, SF), :]
            n = (features_first(half * N + c) * scale) * jnp.concatenate([g, g, g], axis=1)
            if half == 0:
                head = n
        ns0[c] = jnp.concatenate([head, n], axis=0).astype(BF16)
        return 0

    def normalise_rows(j, _):
        at = pl.ds(pl.multiple_of(j * 48, 48), 48)
        sc = scol[at, :]
        for h in (0, 1):
            for c in range(5):
                x = xs[2 * N + h * N + j, c * 48:(c + 1) * 48, :].astype(F32)
                n = (x * sc) * grow[h, 0:1, c * 128:(c + 1) * 128]
                ns1[h, at, c * 128:(c + 1) * 128] = n.astype(BF16)
        return 0

    lax.fori_loop(0, N, normalise, 0)
    lax.fori_loop(0, N, normalise_rows, 0)

    ls[...] = dot(wst0[...], ns0[...].reshape(N * TF, TOK))
    ls[...] += dot_rows(wst1[0], ns1[0])
    ls[...] += dot_rows(wst1[1], ns1[1])

    step_rows = 32

    def fold(x):
        out = x[0:8]
        for j in range(1, step_rows // 8):
            out = out + x[j * 8:(j + 1) * 8]
        return out

    zero = jnp.zeros((8, TOK), F32)

    def student(i, carry):
        at = pl.ds(pl.multiple_of(i * step_rows, step_rows), step_rows)
        logit = ls[at, :]
        pupil = 30.0 * jnp.tanh(logit / 30.0)
        e = jnp.exp(pupil - 30.0)
        slope = 1.0 - (pupil / 30.0) ** 2
        pu[at, :], ep[at, :], qq[at, :] = pupil, e, slope
        sl = slope * logit
        ql[at, :] = sl
        return carry[0] + fold(e), carry[1] + fold(e * sl)

    zs8, u8 = lax.fori_loop(0, VOC // step_rows, student, (zero, zero))

    all_from_sibling(1)

    @pl.when(first)
    def _():
        teacher_dots(1)

    @pl.when(jnp.logical_not(first))
    def _():
        teacher_dots(0)


    def teacher(i, carry):
        at = pl.ds(pl.multiple_of(i * step_rows, step_rows), step_rows)
        teach = 30.0 * jnp.tanh(lt[at, :] / 30.0)
        e = jnp.exp(teach - 30.0)
        et[at, :] = e
        return (
            carry[0] + fold(e),
            carry[1] + fold(e * (teach - pu[at, :])),
            carry[2] + fold(e * ql[at, :]),
        )

    zt8, c8, v8 = lax.fori_loop(0, VOC // step_rows, teacher, (zero, zero, zero))
    fold8 = [jnp.sum(t, axis=0, keepdims=True) for t in (zt8, zs8, c8, u8, v8)]
    main_sums = jnp.concatenate(fold8[:2], axis=0)
    late_sums = jnp.concatenate(fold8[2:] + [jnp.zeros((1, TOK), F32)], axis=0)

    def line_start(buf, send, recv, k, here, who, value):
        buf[here] = value
        for j in far_first:
            i = k * N + j
            copy = remote(buf.at[here], buf.at[here], send.at[i], recv.at[i], who((here + j) % N))
            copy.start()
            sent.append(copy)

    def line_end(buf, send, recv, k, here):
        for j in range(1, N):
            i, at = k * N + j, (here + N - j) % N
            remote(buf.at[at], buf.at[at], send.at[i], recv.at[i], sibling).wait_recv()
        out = buf[0]
        for j in range(1, N):
            out = out + buf[j]
        return out

    others = [(dh, da, dc) for dh in (1, 0) for da in (1, 0) for dc in (0, 1) if dh or da or dc]

    def x_start(buf, k, value):
        here = (xh * 2 + xl) * 2 + s
        buf[here] = value
        for j, (dh, da, dc) in enumerate(others):
            i = k * 7 + j
            copy = remote(
                buf.at[here], buf.at[here], x_send.at[i], x_recv.at[i], dev(xl ^ da, y, xh ^ dh, z, s ^ dc)
            )
            copy.start()
            sent.append(copy)

    def x_end(buf, k):
        for j, (dh, da, dc) in enumerate(others):
            i, at = k * 7 + j, ((xh ^ dh) * 2 + (xl ^ da)) * 2 + (s ^ dc)
            remote(buf.at[at], buf.at[at], x_send.at[i], x_recv.at[i], sibling).wait_recv()
        out = buf[0]
        for j in range(1, 8):
            out = out + buf[j]
        return out

    def along_z(t):
        return dev(xl, y, xh, t, s)

    def along_y(t):
        return dev(xl, t, xh, z, s)

    line_start(s_z, z_send, z_recv, 0, z, along_z, main_sums)
    value = line_end(s_z, z_send, z_recv, 0, z)
    line_start(s_y, y_send, y_recv, 0, y, along_y, value)
    line_start(d_z, z_send, z_recv, 1, z, along_z, late_sums)
    value = line_end(s_y, y_send, y_recv, 0, y)
    x_start(s_x, 0, value)
    late_value = line_end(d_z, z_send, z_recv, 1, z)
    line_start(d_y, y_send, y_recv, 1, y, along_y, late_value)
    value = x_end(s_x, 0)
    zt, zs = value[0:1], value[1:2]

    maskf = jnp.broadcast_to(mask[...].astype(F32).reshape(1, TOK), (16, TOK)).astype(BF16)
    maskf = dot(maskf, perm[...])[0:1]
    weight = maskf / jnp.maximum(jnp.sum(maskf, axis=1, keepdims=True), 1.0)
    over_s, over_t = weight / zs, weight / zt

    def gradient(i, _):
        at = pl.ds(pl.multiple_of(i * step_rows, step_rows), step_rows)
        dpu[at, :] = ((ep[at, :] * over_s - et[at, :] * over_t) * qq[at, :]).astype(BF16)
        return 0

    lax.fori_loop(0, VOC // step_rows, gradient, 0)

    offsets = (4, 3, -3, 2, -2, 1, -1, 0)
    w_all = dpu[...]

    def chunk(i):
        off = offsets[i]
        g_out[i] = dot(wsr[(1 - s) * N + (q + off + N) % N], w_all).astype(BF16)
        copy = remote(g_out.at[i], g_in.at[i], gs_send.at[i], gs_recv.at[i], sibling)
        copy.start()
        sent.append(copy)
        g_own[i] = dot(wsr[s * N + (p + off + N) % N], w_all)

    def own(i):
        remote(g_out.at[i], g_in.at[i], gs_send.at[i], gs_recv.at[i], sibling).wait_recv()
        g_own[i] = g_own[i] + g_in[i].astype(F32)

    spare = jnp.zeros((SP - SF, TOK), F32)

    def keeper(half, place):
        a = jnp.where(xh == half, xl, 1 - xl)
        return dev(a, jnp.where(first, y, place), half, jnp.where(first, place, z), s)

    def give(way, dist, half, i):
        at = (way * 4 + dist - 1) * 2
        value = g_own[i, half * SF:(half + 1) * SF, :]
        if dist == 2:
            value = value + take(way, 3, half)
            if half == way:
                value = value + take(way, 4, half)
        r_out[at + half] = jnp.concatenate([value, spare], axis=0).astype(BF16)
        place = (p + (N - dist if way else dist)) % N
        if dist != 2:
            to, land = ((right, left), (right2, left2))[dist == 4][way], half
        else:
            to, land = keeper(half, place), jnp.where(xh == half, 0, 1)
        copy = remote(r_out.at[at + half], r_in.at[at + land], rr_send.at[at + half], rr_recv.at[at + land], to)
        copy.start()
        sent.append(copy)

    def take(way, dist, land):
        at = (way * 4 + dist - 1) * 2 + land
        remote(r_out.at[at], r_in.at[at], rr_send.at[at], rr_recv.at[at], sibling).wait_recv()
        return r_in[at].astype(F32)[:SF]

    right2, left2 = ring((p + 2) % N), ring((p + N - 2) % N)
    chunk(0)
    chunk(1)
    chunk(2)
    own(0)
    give(0, 4, 0, 0)
    give(1, 4, 1, 0)
    own(1)
    give(0, 3, 1, 1)
    own(2)
    give(1, 3, 0, 2)
    give(0, 3, 0, 1)
    give(1, 3, 1, 2)
    for i in range(3, 8):
        chunk(i)
    own(5)
    own(6)
    own(7)
    for half in (0, 1):
        give(0, 1, half, 5)
        give(1, 1, half, 6)
    own(3)
    own(4)

    late_value = line_end(d_y, y_send, y_recv, 1, y)
    x_start(d_x, 1, late_value)
    @pl.when(first)
    def _():
        held[...] = features_first(xh * N + p) * scale

    @pl.when(jnp.logical_not(first))
    def _():
        for c in range(5):
            x = xs[pl.ds(2 * N + xh * N, N), c * 48:(c + 1) * 48, :].reshape(TOK, 128).astype(F32)
            xturn[c * 128:(c + 1) * 128, :] = x.T
        held[...] = xturn[pl.ds(pl.multiple_of(p * SF, 8), SF), :] * scale

    give(0, 2, 1, 3)
    give(1, 2, 0, 4)
    give(0, 2, 0, 3)
    give(1, 2, 1, 4)
    for half in (0, 1):
        near = g_own[7, half * SF:(half + 1) * SF, :] + take(0, 1, half) + take(1, 1, half)
        g_own[7, half * SF:(half + 1) * SF, :] = near
    other = g_own[7, pl.ds(pl.multiple_of((1 - xh) * SF, 8), SF), :]
    e_out[...] = jnp.concatenate([other, spare], axis=0).astype(BF16)
    e_copy = remote(e_out, e_in, e_send.at[0], e_recv.at[0], across)
    e_copy.start()
    sent.append(e_copy)
    keep = g_own[7, pl.ds(pl.multiple_of(xh * SF, 8), SF), :]
    e_copy.wait_recv()
    keep = keep + e_in[...].astype(F32)[:SF]
    late_value = x_end(d_x, 1)
    rowdot = (late_value[1:2] * over_s - late_value[2:3] * over_t) / scale
    stacked = jnp.concatenate([scale, rowdot, jnp.zeros((126, TOK), F32)], axis=0)
    cols[...] = stacked.T
    for land in (0, 1):
        for way in (0, 1):
            keep = keep + take(way, 2, land)

    x_held = held[...]
    gains = gb[pl.ds(pl.multiple_of(v * SF, 8), SF), :]
    filler = jnp.zeros((128 - SF, 128), F32)
    gain_row = jnp.concatenate([gains, filler], axis=0).T[:ROWS]
    mycols = cols[pl.ds(pl.multiple_of((y * 2 + xl) * ROWS, 8), ROWS), :]
    my_scale, my_rowdot = mycols[:, 0:1], mycols[:, 1:2]
    gain_grad = jnp.sum(keep * x_held, axis=1, keepdims=True)
    gain_grad = jnp.concatenate([jnp.broadcast_to(gain_grad, (SF, 128)), filler], axis=0).T[:8]
    rough = gain_grad.astype(BF16).astype(F32)
    row = lax.broadcasted_iota(jnp.int32, (8, 128), 0)
    gain_grad = jnp.where(row == 0, rough, gain_grad - rough)
    keep = jnp.concatenate([keep, jnp.zeros((128 - SF, TOK), F32)], axis=0).T
    for m in range(2 * N):
        at = ((m % N) * 2 + m // N) * ROWS
        f_out[m] = jnp.concatenate([keep[at:at + ROWS], gain_grad], axis=0).astype(BF16)

    token_kl = late_value[0:1] / zt - jnp.log(zt) + jnp.log(zs)

    def final_send(m):
        return remote(f_out.at[m], f_in.at[slot], f_send.at[m], f_recv.at[slot], owner(m))

    def is_other(m):
        who = owner(m)
        return jnp.logical_not(jnp.logical_and(who[0] == d, who[1] == v))

    def send_final(i, _):
        m = (d + 1 + i) % (2 * N)

        @pl.when(is_other(m))
        def _():
            final_send(m).start()

        return 0

    lax.fori_loop(0, 2 * N, send_final, 0)

    loss_out[...] = jnp.sum(weight * token_kl, axis=1, keepdims=True)
    rest, split = token_kl, []
    for _ in range(3):
        split.append(rest.astype(BF16).astype(F32))
        rest = rest - split[-1]
    split = jnp.concatenate(split + [jnp.zeros((13, TOK), F32)], axis=0).astype(BF16)
    placed = dot_rows(split, perm[...])
    kl_out[...] = ((placed[0:1] + placed[1:2]) + placed[2:3]).reshape(TOK)

    @pl.when(self_in)
    def _():
        f_in[slot] = f_out[d]

    def wait_final(m, _):
        @pl.when(jnp.logical_not(jnp.logical_and(self_in, m == slot)))
        def _():
            remote(f_out.at[m], f_in.at[m], f_send.at[m], f_recv.at[m], sibling).wait_recv()

        return 0

    lax.fori_loop(0, 2 * N, wait_final, 0)
    got_all = f_in[0].astype(F32)
    for m in range(1, 2 * N):
        got_all = got_all + f_in[m].astype(F32)
    dnormed = got_all[:ROWS]
    x = pad_s[...]
    grad = gain_row * dnormed * my_scale - x * (my_scale**3 * my_rowdot / (SF * 4 * N))
    gh_out[...] = grad[:, :SF]
    gg_out[...] = (got_all[ROWS:ROWS + 1] + got_all[ROWS + 1:ROWS + 2])[:, :SF].reshape(SF)

    for copy in sent:
        copy.wait_send()

    def finish(m, _):
        @pl.when(is_other(m))
        def _():
            final_send(m).wait_send()

        return 0

    lax.fori_loop(0, 2 * N, finish, 0)


def outputs(kl, loss, gh, gg, kl_out, loss_out, gh_out, gg_out):
    kl_out[...] = kl[...]
    loss_out[...] = loss[...]
    gh_out[...] = gh[...]
    gg_out[...] = gg[...]


def on_device(teacher_hidden, teacher_head, student_hidden, student_gain, student_head, token_mask):
    def shape(*dims):
        return jax.ShapeDtypeStruct(dims, F32)

    vmem = pl.BlockSpec(memory_space=pltpu.VMEM)
    anywhere = pl.BlockSpec(memory_space=pl.ANY)

    def half(*dims):
        return pltpu.VMEM(dims, BF16)

    def full(*dims):
        return pltpu.VMEM(dims, F32)

    dma = pltpu.SemaphoreType.DMA
    kl, loss, gh, gg = pl.pallas_call(
        body,
        out_shape=(shape(TOK), shape(1, 1), shape(ROWS, SF), shape(SF)),
        in_specs=[vmem, vmem, vmem, vmem, anywhere, anywhere],
        out_specs=(vmem, vmem, vmem, vmem),
        scratch_shapes=[
            half(4608, VOC), half(2304, VOC),
            half(4, VOC, 1152), half(VOC, 1152), half(2, VOC, 640), half(16, TF, VOC),
            full(2304, 128), full(2, 8, 640), half(TOK, TOK),
            full(ROWS, 256), full(ROWS, 128),
            half(2 * ROWS, 128), half(32, 2 * ROWS, 128),
            half(32, 3 * TF, 128), half(32, 3 * SP, 128),
            half(N, TF, TOK), half(2, TOK, 640), full(TOK, 128), full(TOK, 128),
            full(VOC, TOK), full(VOC, TOK), full(VOC, TOK), full(VOC, TOK),
            full(VOC, TOK), full(VOC, TOK), full(VOC, TOK), half(VOC, TOK),
            full(N, 2, TOK), full(N, 2, TOK), full(8, 2, TOK),
            full(N, 4, TOK), full(N, 4, TOK), full(8, 4, TOK),
            full(TOK, 128), full(640, TOK), full(SF, TOK),
            full(8, TF, TOK), half(8, TF, TOK), half(8, TF, TOK),
            half(16, SP, TOK), half(16, SP, TOK),
            half(SP, TOK), half(SP, TOK),
            half(16, 32, 128), half(16, 32, 128),
            dma((2,)), dma((31,)), dma((31,)),
            dma((64,)), dma((64,)), dma((32,)), dma((32,)),
            dma((16,)), dma((16,)), dma((16,)), dma((16,)), dma((14,)), dma((14,)),
            dma((8,)), dma((8,)), dma((16,)), dma((16,)), dma((1,)), dma((1,)), dma((16,)), dma((16,)),
        ],
        compiler_params=pltpu.CompilerParams(
            collective_id=0, has_side_effects=True, vmem_limit_bytes=56 * 1024 * 1024
        ),
        name="distill",
    )(
        teacher_hidden, student_hidden, student_gain.reshape(18, 128), token_mask,
        teacher_head, student_head,
    )
    kl, loss, gh, gg = pl.pallas_call(
        outputs,
        out_shape=(shape(TOK), shape(1, 1), shape(ROWS, SF), shape(SF)),
        in_specs=[vmem] * 4,
        out_specs=(vmem,) * 4,
        name="outputs",
    )(kl, loss, gh, gg)
    return kl, loss.reshape(()), gh, gg


def solution(mesh):
    placed = (
        P("dp", "vocab"),
        P(None, ("dp", "vocab")),
        P("dp", "vocab"),
        P(),
        P(None, ("dp", "vocab")),
        P(),
    )
    return jax.shard_map(
        on_device,
        mesh=mesh,
        in_specs=placed,
        out_specs=(P(), P(), P("dp", "vocab"), P("vocab")),
        check_vma=False,
    )
```

```python
import jax
import jax.numpy as jnp
from jax import lax
from jax.experimental import pallas as pl
from jax.experimental.pallas import tpu as pltpu
from jax.sharding import PartitionSpec as P

F32, BF16 = jnp.float32, jnp.bfloat16
MESH = pl.DeviceIdType.MESH
N = 8
TOK, ROWS = 384, 24
TF, SF = 144, 72
SP = 80
VOC = 256
STOP = 99


def body(
    th, sh, gain, mask, wt_hbm, ws_hbm,
    kl_out, loss_out, gh_out, gg_out,
    wt, ws, wtt, wst0, wst1, wsr, gb, grow, perm, pad_t, pad_s, piece, got, xt, xs, ns0, ns1, sq, scol,
    ls, lt, pu, ep, qq, ql, et, dpu, s_z, s_y, s_x, d_z, d_y, d_x, cols, xturn, held,
    g_own, g_out, g_in, r_out, r_in, e_out, e_in, f_out, f_in,
    w_sem, p_send, p_recv, ring_send, ring_recv, sib_send, sib_recv,
    z_send, z_recv, y_send, y_recv, x_send, x_recv,
    gs_send, gs_recv, rr_send, rr_recv, e_send, e_recv, f_send, f_recv,
):
    d, v = lax.axis_index("dp"), lax.axis_index("vocab")
    xl, y = d // N, d % N
    s, z, xh = v % 2, (v // 2) % N, v // (2 * N)
    first = s == 0
    p = jnp.where(first, z, y)
    q = jnp.where(first, y, z)

    def dev(xl, y, xh, z, s):
        return (xl * N + y, (xh * N + z) * 2 + s)

    def ring(place):
        return dev(xl, jnp.where(first, y, place), xh, jnp.where(first, place, z), s)

    def member(dh, da, dj):
        j = (q + dj) % N
        return dev(xl ^ da, jnp.where(first, j, y), xh ^ dh, jnp.where(first, z, j), s)

    def owner(m):
        return dev(m // N, m % N, xh, p, s)

    slot = xl * N + q
    far_first = (4, 3, 5, 2, 6, 1, 7)
    line_mates = [
        (dh, da, dj) for dh in (0, 1) for dj in far_first + (0,) for da in (1, 0) if dh or da or dj
    ]
    self_in = jnp.logical_or(first, y == z)
    right, left = ring((p + 1) % N), ring((p + N - 1) % N)
    sibling = dev(xl, y, xh, z, 1 - s)
    across = dev(1 - xl, y, 1 - xh, z, s)

    def remote(src, dst, send, recv, to):
        return pltpu.make_async_remote_copy(
            src_ref=src, dst_ref=dst, send_sem=send, recv_sem=recv, device_id=to, device_id_type=MESH
        )

    wt_copy = pltpu.make_async_copy(wt_hbm, wt, w_sem.at[0])
    ws_copy = pltpu.make_async_copy(ws_hbm, ws, w_sem.at[1])
    wt_copy.start()
    ws_copy.start()

    barrier = pltpu.get_barrier_semaphore()

    def tell(to):
        pl.semaphore_signal(barrier, inc=1, device_id=to, device_id_type=MESH)

    for mate in line_mates:
        tell(member(*mate))
    for to in (right, left, sibling):
        tell(to)

    pad_t[...] = jnp.zeros_like(pad_t)
    pad_s[...] = jnp.zeros_like(pad_s)
    pad_t[:, :TF] = th[...].astype(F32)
    pad_s[:, :SF] = sh[...].astype(F32)
    lane = lax.broadcasted_iota(jnp.int32, (ROWS, 128), 1)
    low = jnp.where(lane < TF - 128, pad_t[:, 128:256], pltpu.roll(pad_s[...], TF - 128, 1))
    piece[...] = jnp.concatenate([pad_t[:, :128], low], axis=0).astype(BF16)

    got[xh * 2 * N + slot] = piece[...]
    pl.semaphore_wait(barrier, len(line_mates) + 3)
    sent = []

    def drain(count):
        for copy in sent[:count]:
            copy.wait_send()
        del sent[:count]


    for i, mate in enumerate(line_mates):
        copy = remote(piece, got.at[xh * 2 * N + slot], p_send.at[i], p_recv.at[i], member(*mate))
        copy.start()
        sent.append(copy)

    def wait_pieces(half):
        for i, (dh, da, dj) in enumerate(line_mates):
            if dh == half:
                at = ((xh ^ dh) * 2 + (xl ^ da)) * N + (q + N - dj) % N
                remote(piece, got.at[at], p_send.at[i], p_recv.at[i], sibling).wait_recv()

    for i in range(18):
        gb[i * 128:(i + 1) * 128, :] = jnp.broadcast_to(gain[i:i + 1, :], (128, 128)).T
    ws_copy.wait()

    def reorder(c, _):
        one = ws[pl.ds(pl.multiple_of(c * TF, 16), TF), :].astype(F32)
        two = ws[pl.ds(pl.multiple_of((N + c) * TF, 16), TF), :].astype(F32)
        wsr[c] = jnp.concatenate([one[:SF], two[:SF]], axis=0).astype(BF16)
        wsr[N + c] = jnp.concatenate([one[SF:], two[SF:]], axis=0).astype(BF16)
        return 0

    lax.fori_loop(0, N, reorder, 0)

    for j in range(9):
        block = wsr[0:N].reshape(N * TF, VOC)[j * 128:(j + 1) * 128]
        wst0[:, j * 128:(j + 1) * 128] = block.T
    for h in (0, 1):
        rows = [wsr[N + c].astype(F32)[h * SF:(h + 1) * SF] for c in range(N)]
        rows = jnp.concatenate(rows + [jnp.zeros((64, VOC), F32)], axis=0).astype(BF16)
        gains = [gb[((h * N + c) * 2 + 1) * SF:((h * N + c) * 2 + 2) * SF, :] for c in range(N)]
        gains = jnp.concatenate(gains + [jnp.zeros((64, 128), F32)], axis=0)
        for j in range(5):
            at = slice(j * 128, (j + 1) * 128)
            wst1[h, :, at] = rows[at].T
            grow[h, :, at] = gains[at].T[:8]

    at = lax.broadcasted_iota(jnp.int32, (TOK, TOK), 1)
    group_of = (at * 2731) >> 16
    token = ((group_of & 1) * N + (group_of >> 1)) * ROWS + (at - group_of * ROWS)
    perm[...] = (token == lax.broadcasted_iota(jnp.int32, (TOK, TOK), 0)).astype(F32).astype(BF16)

    def turn_teacher(i):
        core, h = i // 2, i % 2
        base = [((h * N + c) * 2 + core) * TF for c in range(N)]
        if core == 0:
            rows = jnp.concatenate([wt[b:b + TF, :] for b in base], axis=0)
            blocks = [rows[j * 128:(j + 1) * 128] for j in range(9)]
        else:
            blocks = [wt[b:b + 128, :] for b in base]
            blocks.append(jnp.concatenate([wt[b + 128:b + TF, :] for b in base], axis=0))
        for j, block in enumerate(blocks):
            wtt[i, :, j * 128:(j + 1) * 128] = block.T

    tail = TF - 128

    def assemble(half):
        base, mine = half * 2 * N, s * 2 * N + half * N + p

        @pl.when(first)
        def _():
            pieces = [got[base + a * N + j].astype(F32) for j in range(N) for a in (0, 1)]
            upper = jnp.concatenate([t[:ROWS] for t in pieces], axis=0).T
            lower = jnp.concatenate([t[ROWS:] for t in pieces], axis=0).T
            for c in range(3):
                at = slice(c * 128, (c + 1) * 128)
                xt[mine, c * TF:(c + 1) * TF, :] = jnp.concatenate([upper[:, at], lower[:tail, at]], axis=0).astype(BF16)
                xs[mine, c * SP:(c + 1) * SP, :] = lower[tail:tail + SP, at].astype(BF16)

        @pl.when(jnp.logical_not(first))
        def _():
            lanes = lax.broadcasted_iota(jnp.int32, (2 * ROWS, 128), 1)
            blank = jnp.zeros((2 * ROWS, 128), F32)
            rest, student = blank, [blank] * 5
            for j in range(N):
                one, two = got[base + j].astype(F32), got[base + N + j].astype(F32)
                upper = jnp.concatenate([one[:ROWS], two[:ROWS]], axis=0)
                lower = jnp.concatenate([one[ROWS:], two[ROWS:]], axis=0)
                xt[mine, j * 48:(j + 1) * 48, :] = upper.astype(BF16)
                turned = pltpu.roll(lower, tail * j, 1) if j else lower
                rest = jnp.where(jnp.logical_and(lanes >= tail * j, lanes < tail * (j + 1)), turned, rest)
                a, b = SF * j // 128, SF * j % 128
                turned = pltpu.roll(lower, (b - tail) % 128, 1) if b != tail else lower
                student[a] = jnp.where(jnp.logical_and(lanes >= b, lanes < b + SF), turned, student[a])
                if b + SF > 128:
                    student[a + 1] = jnp.where(lanes < b + SF - 128, turned, student[a + 1])
            xt[mine, 8 * 48:9 * 48, :] = rest.astype(BF16)
            for c in range(5):
                xs[mine, c * 48:(c + 1) * 48, :] = student[c].astype(BF16)

    def unit(core, place, other, part):
        i = core * 2 * N + (1 - xh if other else xh) * N + place
        if part == 0:
            return xs.at[i]
        return xt.at[i] if part == 4 else xt.at[i, (part - 1) * TF:part * TF]

    def push(ref, send, recv, to):
        copy = remote(ref, ref, send, recv, to)
        copy.start()
        sent.append(copy)

    def to_ring(way, step, other, part, place):
        i = (way * 4 + step) * 8 + other * 4 + part
        push(unit(s, place, other, part), ring_send.at[i], ring_recv.at[i], (right, left)[way])

    def from_ring(way, step, other, part, place):
        i = (way * 4 + step) * 8 + other * 4 + part
        ref = unit(s, place, other, part)
        remote(ref, ref, ring_send.at[i], ring_recv.at[i], sibling).wait_recv()

    def to_sibling(slot, other, part, place):
        if part in (0, 3):
            i = slot * 4 + other * 2 + part // 3
            push(unit(s, place, other, part and 4), sib_send.at[i], sib_recv.at[i], sibling)

    def from_sibling(slot, other, kind, place):
        i = slot * 4 + other * 2 + kind
        ref = unit(1 - s, place, other, kind * 4)
        remote(ref, ref, sib_send.at[i], sib_recv.at[i], sibling).wait_recv()

    def behind(place, way, step):
        return (place + (N - step if way == 0 else step)) % N

    def start_ring(other):
        for part in range(4):
            to_ring(0, 0, other, part, p)
            to_ring(1, 0, other, part, p)
            to_sibling(0, other, part, p)

    def go_round(step, other):
        for part in range(4):
            for way in (0, 1):
                place = behind(p, way, step)
                from_ring(way, step - 1, other, part, place)
                if step < 3 or other == way:
                    to_ring(way, step, other, part, place)
                to_sibling(way * 3 + step, other, part, place)

    wait_pieces(0)
    assemble(xh)
    start_ring(0)
    wait_pieces(1)
    assemble(1 - xh)
    start_ring(1)
    wt_copy.wait()
    turn_teacher(0)
    go_round(1, 0)
    go_round(1, 1)
    turn_teacher(1)
    go_round(2, 0)
    go_round(2, 1)
    turn_teacher(2)
    go_round(3, 0)
    go_round(3, 1)
    turn_teacher(3)

    far, sib_far = behind(p, 0, 4), behind(q, 0, 4)

    def last(parts):
        for part in parts:
            for way in (0, 1):
                from_ring(way, 3, way, part, far)
                to_sibling(7, way, part, far)

    def all_from_sibling(kind):
        for other in (0, 1):
            from_sibling(0, other, kind, q)
            for step in (1, 2, 3):
                for way in (0, 1):
                    from_sibling(way * 3 + step, other, kind, behind(q, way, step))
            from_sibling(7, other, kind, sib_far)

    def dot(a, b):
        return jnp.dot(a, b, preferred_element_type=F32)

    def dot_rows(a, b):
        return lax.dot_general(a, b, (((1,), (1,)), ((), ())), preferred_element_type=F32)

    def tokens_last(h):
        cs = [xt[h * N:(h + 1) * N, c * TF:(c + 1) * TF, :].reshape(N * TF, 128) for c in range(3)]
        return jnp.concatenate(cs, axis=1)

    def tokens_first(h):
        at = 2 * N + h * N
        cs = [xt[at:at + N, c * 48:(c + 1) * 48, :].reshape(TOK, 128) for c in range(9)]
        return jnp.concatenate(cs, axis=1)

    def teacher_dots(core):
        for h in (0, 1):
            lt[...] += dot_rows(wtt[2 + h], tokens_first(h)) if core else dot(wtt[h], tokens_last(h))

    last((0, 1, 2, 3))
    lt[...] = jnp.zeros_like(lt)

    @pl.when(first)
    def _():
        teacher_dots(0)

    @pl.when(jnp.logical_not(first))
    def _():
        teacher_dots(1)

    all_from_sibling(0)

    def squares(i, total):
        parts = []
        for c in range(3):
            x = xs[i, c * SP:(c + 1) * SP, :].astype(F32)
            part = x[0:8] * x[0:8]
            for j in range(1, SF // 8):
                part = part + x[j * 8:(j + 1) * 8] * x[j * 8:(j + 1) * 8]
            parts.append(part)
        return total + jnp.concatenate(parts, axis=1)

    def squares_rows(j, _):
        part = jnp.zeros((48, 128), F32)
        for h in (0, 1):
            for c in range(5):
                x = xs[2 * N + h * N + j, c * 48:(c + 1) * 48, :].astype(F32)
                part = part + x * x
        sq[pl.ds(pl.multiple_of(j * 48, 48), 48), :] = part
        return 0

    total = lax.fori_loop(0, 2 * N, squares, jnp.zeros((8, TOK), F32))
    lax.fori_loop(0, N, squares_rows, 0)
    total = jnp.sum(total, axis=0, keepdims=True) + jnp.sum(sq[...].T, axis=0, keepdims=True)
    scale = lax.rsqrt(total / (SF * 4 * N) + 1e-6)
    scol[...] = jnp.broadcast_to(scale, (128, TOK)).T

    def features_first(i):
        x = xs[i].astype(F32)
        return jnp.concatenate([x[c * SP:c * SP + SF] for c in range(3)], axis=1)

    def normalise(c, _):
        for half in (0, 1):
            at = pl.multiple_of((half * N + c) * 2 * SF, 8)
            g = gb[pl.ds(at, SF), :]
            n = (features_first(half * N + c) * scale) * jnp.concatenate([g, g, g], axis=1)
            if half == 0:
                head = n
        ns0[c] = jnp.concatenate([head, n], axis=0).astype(BF16)
        return 0

    def normalise_rows(j, _):
        at = pl.ds(pl.multiple_of(j * 48, 48), 48)
        sc = scol[at, :]
        for h in (0, 1):
            for c in range(5):
                x = xs[2 * N + h * N + j, c * 48:(c + 1) * 48, :].astype(F32)
                n = (x * sc) * grow[h, 0:1, c * 128:(c + 1) * 128]
                ns1[h, at, c * 128:(c + 1) * 128] = n.astype(BF16)
        return 0

    lax.fori_loop(0, N, normalise, 0)
    lax.fori_loop(0, N, normalise_rows, 0)

    ls[...] = dot(wst0[...], ns0[...].reshape(N * TF, TOK))
    ls[...] += dot_rows(wst1[0], ns1[0])
    ls[...] += dot_rows(wst1[1], ns1[1])

    step_rows = 32

    def fold(x):
        out = x[0:8]
        for j in range(1, step_rows // 8):
            out = out + x[j * 8:(j + 1) * 8]
        return out

    zero = jnp.zeros((8, TOK), F32)

    def student(i, carry):
        at = pl.ds(pl.multiple_of(i * step_rows, step_rows), step_rows)
        logit = ls[at, :]
        bent = jnp.tanh(logit * (1.0 / 30.0))
        pupil = 30.0 * bent
        e = jnp.exp(pupil - 30.0)
        slope = 1.0 - bent * bent
        pu[at, :], ep[at, :], qq[at, :] = pupil, e, slope
        sl = slope * logit
        ql[at, :] = sl
        return carry[0] + fold(e), carry[1] + fold(e * sl)

    zs8, u8 = lax.fori_loop(0, VOC // step_rows, student, (zero, zero))

    all_from_sibling(1)

    @pl.when(first)
    def _():
        teacher_dots(1)

    @pl.when(jnp.logical_not(first))
    def _():
        teacher_dots(0)


    def teacher(i, carry):
        at = pl.ds(pl.multiple_of(i * step_rows, step_rows), step_rows)
        teach = 30.0 * jnp.tanh(lt[at, :] * (1.0 / 30.0))
        e = jnp.exp(teach - 30.0)
        et[at, :] = e
        return (
            carry[0] + fold(e),
            carry[1] + fold(e * (teach - pu[at, :])),
            carry[2] + fold(e * ql[at, :]),
        )

    zt8, c8, v8 = lax.fori_loop(0, VOC // step_rows, teacher, (zero, zero, zero))
    fold8 = [jnp.sum(t, axis=0, keepdims=True) for t in (zt8, zs8, c8, u8, v8)]
    main_sums = jnp.concatenate(fold8[:2], axis=0)
    late_sums = jnp.concatenate(fold8[2:] + [jnp.zeros((1, TOK), F32)], axis=0)

    def line_start(buf, send, recv, k, here, who, value):
        buf[here] = value
        for j in far_first:
            i = k * N + j
            copy = remote(buf.at[here], buf.at[here], send.at[i], recv.at[i], who((here + j) % N))
            copy.start()
            sent.append(copy)

    def line_end(buf, send, recv, k, here):
        for j in range(1, N):
            i, at = k * N + j, (here + N - j) % N
            remote(buf.at[at], buf.at[at], send.at[i], recv.at[i], sibling).wait_recv()
        out = buf[0]
        for j in range(1, N):
            out = out + buf[j]
        return out

    others = [(dh, da, dc) for dh in (1, 0) for da in (1, 0) for dc in (0, 1) if dh or da or dc]

    def x_start(buf, k, value):
        here = (xh * 2 + xl) * 2 + s
        buf[here] = value
        for j, (dh, da, dc) in enumerate(others):
            i = k * 7 + j
            copy = remote(
                buf.at[here], buf.at[here], x_send.at[i], x_recv.at[i], dev(xl ^ da, y, xh ^ dh, z, s ^ dc)
            )
            copy.start()
            sent.append(copy)

    def x_end(buf, k):
        for j, (dh, da, dc) in enumerate(others):
            i, at = k * 7 + j, ((xh ^ dh) * 2 + (xl ^ da)) * 2 + (s ^ dc)
            remote(buf.at[at], buf.at[at], x_send.at[i], x_recv.at[i], sibling).wait_recv()
        out = buf[0]
        for j in range(1, 8):
            out = out + buf[j]
        return out

    def along_z(t):
        return dev(xl, y, xh, t, s)

    def along_y(t):
        return dev(xl, t, xh, z, s)

    old = len(sent)
    line_start(s_z, z_send, z_recv, 0, z, along_z, main_sums)
    drain(old)
    value = line_end(s_z, z_send, z_recv, 0, z)
    old = len(sent)
    line_start(s_y, y_send, y_recv, 0, y, along_y, value)
    line_start(d_z, z_send, z_recv, 1, z, along_z, late_sums)
    drain(old)
    value = line_end(s_y, y_send, y_recv, 0, y)
    old = len(sent)
    x_start(s_x, 0, value)
    drain(old)
    late_value = line_end(d_z, z_send, z_recv, 1, z)
    line_start(d_y, y_send, y_recv, 1, y, along_y, late_value)
    value = x_end(s_x, 0)
    zt, zs = value[0:1], value[1:2]

    maskf = jnp.broadcast_to(mask[...].astype(F32).reshape(1, TOK), (16, TOK)).astype(BF16)
    maskf = dot(maskf, perm[...])[0:1]
    weight = maskf / jnp.maximum(jnp.sum(maskf, axis=1, keepdims=True), 1.0)
    over_s, over_t = weight / zs, weight / zt

    def gradient(i, _):
        at = pl.ds(pl.multiple_of(i * step_rows, step_rows), step_rows)
        dpu[at, :] = ((ep[at, :] * over_s - et[at, :] * over_t) * qq[at, :]).astype(BF16)
        return 0

    lax.fori_loop(0, VOC // step_rows, gradient, 0)

    offsets = (4, 3, -3, 2, -2, 1, -1, 0)
    w_all = dpu[...]

    def chunk(i):
        off = offsets[i]
        g_out[i] = dot(wsr[(1 - s) * N + (q + off + N) % N], w_all).astype(BF16)
        copy = remote(g_out.at[i], g_in.at[i], gs_send.at[i], gs_recv.at[i], sibling)
        copy.start()
        sent.append(copy)
        g_own[i] = dot(wsr[s * N + (p + off + N) % N], w_all)

    def own(i):
        remote(g_out.at[i], g_in.at[i], gs_send.at[i], gs_recv.at[i], sibling).wait_recv()
        g_own[i] = g_own[i] + g_in[i].astype(F32)

    spare = jnp.zeros((SP - SF, TOK), F32)

    def keeper(half, place):
        a = jnp.where(xh == half, xl, 1 - xl)
        return dev(a, jnp.where(first, y, place), half, jnp.where(first, place, z), s)

    def give(way, dist, half, i):
        at = (way * 4 + dist - 1) * 2
        value = g_own[i, half * SF:(half + 1) * SF, :]
        if dist == 2:
            value = value + take(way, 3, half)
            if half == way:
                value = value + take(way, 4, half)
        r_out[at + half] = jnp.concatenate([value, spare], axis=0).astype(BF16)
        place = (p + (N - dist if way else dist)) % N
        if dist != 2:
            to, land = ((right, left), (right2, left2))[dist == 4][way], half
        else:
            to, land = keeper(half, place), jnp.where(xh == half, 0, 1)
        copy = remote(r_out.at[at + half], r_in.at[at + land], rr_send.at[at + half], rr_recv.at[at + land], to)
        copy.start()
        sent.append(copy)

    def take(way, dist, land):
        at = (way * 4 + dist - 1) * 2 + land
        remote(r_out.at[at], r_in.at[at], rr_send.at[at], rr_recv.at[at], sibling).wait_recv()
        return r_in[at].astype(F32)[:SF]

    right2, left2 = ring((p + 2) % N), ring((p + N - 2) % N)
    chunk(0)
    chunk(1)
    chunk(2)
    own(0)
    give(0, 4, 0, 0)
    give(1, 4, 1, 0)
    own(1)
    give(0, 3, 1, 1)
    own(2)
    give(1, 3, 0, 2)
    give(0, 3, 0, 1)
    give(1, 3, 1, 2)
    chunk(5)
    chunk(6)
    chunk(3)
    own(5)
    own(6)
    for half in (0, 1):
        give(0, 1, half, 5)
        give(1, 1, half, 6)
    chunk(4)
    chunk(7)
    own(7)
    own(3)
    own(4)

    late_value = line_end(d_y, y_send, y_recv, 1, y)
    old = len(sent) - 10
    x_start(d_x, 1, late_value)
    drain(old)
    @pl.when(first)
    def _():
        held[...] = features_first(xh * N + p) * scale

    @pl.when(jnp.logical_not(first))
    def _():
        for c in range(5):
            x = xs[pl.ds(2 * N + xh * N, N), c * 48:(c + 1) * 48, :].reshape(TOK, 128).astype(F32)
            xturn[c * 128:(c + 1) * 128, :] = x.T
        held[...] = xturn[pl.ds(pl.multiple_of(p * SF, 8), SF), :] * scale

    give(0, 2, 1, 3)
    give(1, 2, 0, 4)
    give(0, 2, 0, 3)
    give(1, 2, 1, 4)
    for half in (0, 1):
        near = g_own[7, half * SF:(half + 1) * SF, :] + take(0, 1, half) + take(1, 1, half)
        g_own[7, half * SF:(half + 1) * SF, :] = near
    other = g_own[7, pl.ds(pl.multiple_of((1 - xh) * SF, 8), SF), :]
    e_out[...] = jnp.concatenate([other, spare], axis=0).astype(BF16)
    e_copy = remote(e_out, e_in, e_send.at[0], e_recv.at[0], across)
    e_copy.start()
    sent.append(e_copy)
    keep = g_own[7, pl.ds(pl.multiple_of(xh * SF, 8), SF), :]
    e_copy.wait_recv()
    keep = keep + e_in[...].astype(F32)[:SF]
    late_value = x_end(d_x, 1)
    rowdot = (late_value[1:2] * over_s - late_value[2:3] * over_t) / scale
    stacked = jnp.concatenate([scale, rowdot, jnp.zeros((126, TOK), F32)], axis=0)
    cols[...] = stacked.T
    for land in (0, 1):
        for way in (0, 1):
            keep = keep + take(way, 2, land)

    x_held = held[...]
    gains = gb[pl.ds(pl.multiple_of(v * SF, 8), SF), :]
    filler = jnp.zeros((128 - SF, 128), F32)
    gain_row = jnp.concatenate([gains, filler], axis=0).T[:ROWS]
    mycols = cols[pl.ds(pl.multiple_of((y * 2 + xl) * ROWS, 8), ROWS), :]
    my_scale, my_rowdot = mycols[:, 0:1], mycols[:, 1:2]
    gain_grad = jnp.sum(keep * x_held, axis=1, keepdims=True)
    gain_grad = jnp.concatenate([jnp.broadcast_to(gain_grad, (SF, 128)), filler], axis=0).T[:8]
    rough = gain_grad.astype(BF16).astype(F32)
    row = lax.broadcasted_iota(jnp.int32, (8, 128), 0)
    gain_grad = jnp.where(row == 0, rough, gain_grad - rough)
    keep = jnp.concatenate([keep, jnp.zeros((128 - SF, TOK), F32)], axis=0).T
    for m in range(2 * N):
        at = ((m % N) * 2 + m // N) * ROWS
        f_out[m] = jnp.concatenate([keep[at:at + ROWS], gain_grad], axis=0).astype(BF16)

    token_kl = late_value[0:1] / zt - jnp.log(zt) + jnp.log(zs)

    def final_send(i, da, dj):
        a, j = xl ^ da, (y + dj) % N
        return remote(f_out.at[a * N + j], f_in.at[slot], f_send.at[i], f_recv.at[slot], owner(a * N + j))

    ways = [(da, dj) for dj in far_first + (0,) for da in (1, 0) if da or dj]
    old = len(sent)
    for i, way in enumerate(ways):
        copy = final_send(i, *way)
        copy.start()
        sent.append(copy)

    @pl.when(jnp.logical_not(self_in))
    def _():
        final_send(15, 0, 0).start()

    loss_out[...] = jnp.sum(weight * token_kl, axis=1, keepdims=True)
    rest, split = token_kl, []
    for _ in range(3):
        split.append(rest.astype(BF16).astype(F32))
        rest = rest - split[-1]
    split = jnp.concatenate(split + [jnp.zeros((13, TOK), F32)], axis=0).astype(BF16)
    placed = dot_rows(split, perm[...])
    kl_out[...] = ((placed[0:1] + placed[1:2]) + placed[2:3]).reshape(TOK)

    @pl.when(self_in)
    def _():
        f_in[slot] = f_out[d]

    drain(old)

    def wait_final(m, _):
        @pl.when(jnp.logical_not(jnp.logical_and(self_in, m == slot)))
        def _():
            remote(f_out.at[m], f_in.at[m], f_send.at[m], f_recv.at[m], sibling).wait_recv()

        return 0

    lax.fori_loop(0, 2 * N, wait_final, 0)
    got_all = f_in[0].astype(F32)
    for m in range(1, 2 * N):
        got_all = got_all + f_in[m].astype(F32)
    dnormed = got_all[:ROWS]
    x = pad_s[...]
    grad = gain_row * dnormed * my_scale - x * (my_scale**3 * my_rowdot / (SF * 4 * N))
    gh_out[...] = grad[:, :SF]
    gg_out[...] = (got_all[ROWS:ROWS + 1] + got_all[ROWS + 1:ROWS + 2])[:, :SF].reshape(SF)

    drain(len(sent))

    @pl.when(jnp.logical_not(self_in))
    def _():
        final_send(15, 0, 0).wait_send()


def outputs(kl, loss, gh, gg, kl_out, loss_out, gh_out, gg_out):
    kl_out[...] = kl[...]
    loss_out[...] = loss[...]
    gh_out[...] = gh[...]
    gg_out[...] = gg[...]


def on_device(teacher_hidden, teacher_head, student_hidden, student_gain, student_head, token_mask):
    def shape(*dims):
        return jax.ShapeDtypeStruct(dims, F32)

    vmem = pl.BlockSpec(memory_space=pltpu.VMEM)
    anywhere = pl.BlockSpec(memory_space=pl.ANY)

    def half(*dims):
        return pltpu.VMEM(dims, BF16)

    def full(*dims):
        return pltpu.VMEM(dims, F32)

    dma = pltpu.SemaphoreType.DMA
    kl, loss, gh, gg = pl.pallas_call(
        body,
        out_shape=(shape(TOK), shape(1, 1), shape(ROWS, SF), shape(SF)),
        in_specs=[vmem, vmem, vmem, vmem, anywhere, anywhere],
        out_specs=(vmem, vmem, vmem, vmem),
        scratch_shapes=[
            half(4608, VOC), half(2304, VOC),
            half(4, VOC, 1152), half(VOC, 1152), half(2, VOC, 640), half(16, TF, VOC),
            full(2304, 128), full(2, 8, 640), half(TOK, TOK),
            full(ROWS, 256), full(ROWS, 128),
            half(2 * ROWS, 128), half(32, 2 * ROWS, 128),
            half(32, 3 * TF, 128), half(32, 3 * SP, 128),
            half(N, TF, TOK), half(2, TOK, 640), full(TOK, 128), full(TOK, 128),
            full(VOC, TOK), full(VOC, TOK), full(VOC, TOK), full(VOC, TOK),
            full(VOC, TOK), full(VOC, TOK), full(VOC, TOK), half(VOC, TOK),
            full(N, 2, TOK), full(N, 2, TOK), full(8, 2, TOK),
            full(N, 4, TOK), full(N, 4, TOK), full(8, 4, TOK),
            full(TOK, 128), full(640, TOK), full(SF, TOK),
            full(8, TF, TOK), half(8, TF, TOK), half(8, TF, TOK),
            half(16, SP, TOK), half(16, SP, TOK),
            half(SP, TOK), half(SP, TOK),
            half(16, 32, 128), half(16, 32, 128),
            dma((2,)), dma((31,)), dma((31,)),
            dma((64,)), dma((64,)), dma((32,)), dma((32,)),
            dma((16,)), dma((16,)), dma((16,)), dma((16,)), dma((14,)), dma((14,)),
            dma((8,)), dma((8,)), dma((16,)), dma((16,)), dma((1,)), dma((1,)), dma((16,)), dma((16,)),
        ],
        compiler_params=pltpu.CompilerParams(
            collective_id=0, has_side_effects=True, vmem_limit_bytes=56 * 1024 * 1024
        ),
        name="distill",
    )(
        teacher_hidden, student_hidden, student_gain.reshape(18, 128), token_mask,
        teacher_head, student_head,
    )
    kl, loss, gh, gg = pl.pallas_call(
        outputs,
        out_shape=(shape(TOK), shape(1, 1), shape(ROWS, SF), shape(SF)),
        in_specs=[vmem] * 4,
        out_specs=(vmem,) * 4,
        name="outputs",
    )(kl, loss, gh, gg)
    return kl, loss.reshape(()), gh, gg


def solution(mesh):
    placed = (
        P("dp", "vocab"),
        P(None, ("dp", "vocab")),
        P("dp", "vocab"),
        P(),
        P(None, ("dp", "vocab")),
        P(),
    )
    return jax.shard_map(
        on_device,
        mesh=mesh,
        in_specs=placed,
        out_specs=(P(), P(), P("dp", "vocab"), P("vocab")),
        check_vma=False,
    )
```
